32 devices in a mesh: fact: 4 (over x, core), dim: 8 (over z, y).
Axes of the slice: x: 2, y: 2, z: 4, core: 2. Of those that a mesh axis runs over, the one named last changes fastest.
Arguments:
- queries: bfloat16 [8192, 1024], P(('fact', 'dim')), may hold values from -6 to 6
- key_rows: bfloat16 [8192, 1024], P('dim'), may hold values from -6 to 6
- value_rows: bfloat16 [8192, 1024], P('dim'), may hold values from -6 to 6
- cotangent: bfloat16 [8192, 1024], P(('fact', 'dim')), may hold values from -6 to 6
- block_lists: int32 [64, 8], P(('fact', 'dim')), may hold values from 0 to 63, as said below
- tile_lengths: int32 [64], P(('fact', 'dim')), may hold values from 1 to 8, as said below
Outputs:
- attended: bfloat16 [8192, 1024], P(('fact', 'dim'))
- query_grad: bfloat16 [8192, 1024], P(('fact', 'dim'))
- key_grad: bfloat16 [8192, 1024], P('dim', 'fact')
- value_grad: bfloat16 [8192, 1024], P('dim', 'fact')
The draws below stay inside these ranges and needn't reach their ends.
Inputs may be any that keep to these rules, and one draw needn't show every extreme that they name: Rows of block_lists come in aligned groups of 2 rows. The entries of one row lie in different ranges [o * 8, (o + 1) * 8). Within one group, all entries that lie in one such range are the same block. Within each aligned run of 8 groups, the first entries of all rows lie in one common range. Only the first tile_lengths[t] entries of row t of block_lists are used.
All inputs are finite; a program needn't handle non-finite values.
Results may differ from the reference program's by a relative error of at most 0.0056.
Values may be sent and summed in bfloat16 or wider, within the bound.
No kernel may reach another device: no remote copies, remote signals or barrier semaphores. Data moves between devices by JAX's collectives and lax.ppermute only.
A program may use at most 192 MiB of HBM per device.

```python
import math
import jax
import jax.numpy as jnp
from jax import lax

D = 1024
HEADS = 16
HEAD_DIM = 64
TILE = 128
LMAX = 8
TILES_DEV = 2
BLK_DEV = 8
NTILES = 64
FACTS = 8192
NBLK = 64
DROWS = 8192
N_FACT = 4
N_DIM = 8


def row_scales(key, row_count):
    return jnp.exp(jax.random.uniform(key, (row_count, 1), minval=math.log(0.3), maxval=math.log(3.0)))


def draw_queries(key, part):
    scales = row_scales(jax.random.fold_in(key, 2), FACTS)
    base_draw = jax.random.normal(jax.random.fold_in(key, 1), (FACTS, D)) * scales
    return jnp.clip(base_draw, -6.0, 6.0).astype(jnp.bfloat16)


def draw_key_rows(key, part):
    scales = row_scales(jax.random.fold_in(key, 4), DROWS)
    base_draw = jax.random.normal(jax.random.fold_in(key, 3), (DROWS, D)) * scales
    return jnp.clip(base_draw, -6.0, 6.0).astype(jnp.bfloat16)


def draw_block_lists(key, part):
    key_first, key_second, key_third = jax.random.split(jax.random.fold_in(key, 11), 3)
    device_total = N_FACT * N_DIM
    picked = jax.random.randint(key_first, (device_total, N_DIM), 0, BLK_DEV)
    hottest = jax.random.randint(key_second, (N_FACT,), 0, N_DIM)
    hot_device = jnp.repeat(hottest, N_DIM)
    device_of_tile = jnp.arange(NTILES, dtype=jnp.int32) // TILES_DEV
    owner_ids = jnp.arange(N_DIM, dtype=jnp.int32)
    rank_scores = jax.random.randint(key_third, (NTILES, N_DIM), 0, 65536) * N_DIM + owner_ids[None, :]
    rank_scores = jnp.where(owner_ids[None, :] == hot_device[device_of_tile][:, None], -1, rank_scores)
    owner_order = jnp.argsort(rank_scores, axis=1)[:, :LMAX].astype(jnp.int32)
    local_pick = jnp.take_along_axis(picked[device_of_tile], owner_order, axis=1)
    return (owner_order * BLK_DEV + local_pick).astype(jnp.int32)


def draw_tile_lengths(key, part):
    key_first, key_second, key_third = jax.random.split(jax.random.fold_in(key, 23), 3)
    device_caps = jax.random.randint(key_first, (N_FACT * N_DIM,), 1, LMAX + 1)
    device_of_tile = jnp.arange(NTILES, dtype=jnp.int32) // TILES_DEV
    raw_draws = jax.random.randint(key_second, (NTILES,), 0, 65536)
    lengths = 1 + raw_draws % device_caps[device_of_tile]
    forced = jax.random.randint(key_third, (), 0, NTILES)
    return lengths.at[forced].set(LMAX).astype(jnp.int32)


def level_of(key, extent, shards, low, high):
    gain = 1.0
    for dim, parts in shards:
        draws = jax.random.uniform(jax.random.fold_in(jax.random.fold_in(key, 6), dim), (parts,), jnp.float32, low / len(shards), high / len(shards))
        gain = gain * jnp.repeat(jnp.exp(draws), extent[dim] // parts).reshape((-1,) + (1,) * (len(extent) - 1 - dim))
    return gain


def scatter_about(rng, dims, width, reach, cuts=(), kind=jnp.bfloat16):
    values = jax.random.normal(rng, dims, jnp.float32) * width
    if len(cuts) > 0:
        values = level_of(rng, dims, cuts, -0.22, 0.18) * values
    return jnp.clip(values, min=-reach, max=reach).astype(kind)


def setup_inputs(seed: int = 0) -> dict:
    key_of = jax.random.split(jax.random.key(seed), 7)
    queries = draw_queries(jax.random.fold_in(key_of[6], 71), 0)
    key_rows = draw_key_rows(jax.random.fold_in(key_of[6], 71), 0)
    value_rows = scatter_about(key_of[2], (DROWS, D), 1.0, 6.0, ((0, 8),))
    cotangent = scatter_about(key_of[3], (FACTS, D), 1.0, 6.0, ((0, 32),))
    block_lists = draw_block_lists(jax.random.fold_in(key_of[6], 71), 0)
    tile_lengths = draw_tile_lengths(jax.random.fold_in(key_of[6], 71), 0)
    return {"queries": queries, "key_rows": key_rows, "value_rows": value_rows, "cotangent": cotangent, "block_lists": block_lists, "tile_lengths": tile_lengths}


NEG_FILL = -1e30


def reference(queries, key_rows, value_rows, cotangent, block_lists, tile_lengths):
    model_width = queries.shape[1]
    tile_count = queries.shape[0] // TILE
    slot_count = block_lists.shape[1]
    scale = HEAD_DIM ** -0.5
    gathered_key_blocks = key_rows.reshape(NBLK, TILE, model_width)
    gathered_value_blocks = value_rows.reshape(NBLK, TILE, model_width)
    query_tiles = queries.reshape(tile_count, TILE, HEADS, HEAD_DIM)
    grad_tiles = cotangent.reshape(tile_count, TILE, HEADS, HEAD_DIM)

    def one_tile(totals, inputs_step):
        key_total, value_total = totals
        query_one, grad_one, chosen, length = inputs_step
        chosen = chosen.astype(jnp.int32)
        key_one = gathered_key_blocks[chosen].reshape(slot_count * TILE, HEADS, HEAD_DIM).astype(jnp.float32)
        value_one = gathered_value_blocks[chosen].reshape(slot_count * TILE, HEADS, HEAD_DIM).astype(jnp.float32)
        alive_keys = (jnp.arange(slot_count * TILE, dtype=jnp.int32) // TILE) < length
        query_wide = query_one.astype(jnp.float32)
        grad_wide = grad_one.astype(jnp.float32)
        scores = jnp.einsum("qhe,khe->hqk", query_wide, key_one) * scale
        scores = jnp.where(alive_keys[None, None, :], scores, NEG_FILL)
        row_max = jnp.max(scores, axis=-1, keepdims=True)
        expo_terms = jnp.exp(scores - row_max)
        weights = expo_terms / jnp.sum(expo_terms, axis=-1, keepdims=True)
        weights_low = lax.optimization_barrier(weights.astype(jnp.bfloat16)).astype(jnp.float32)
        attended = jnp.einsum("hqk,khe->qhe", weights_low, value_one).astype(jnp.bfloat16)
        dweights = jnp.einsum("qhe,khe->hqk", grad_wide, value_one)
        row_delta = jnp.sum(weights * dweights, axis=-1, keepdims=True)
        dscores = lax.optimization_barrier((weights * (dweights - row_delta)).astype(jnp.bfloat16)).astype(jnp.float32)
        query_grad = (jnp.einsum("hqk,khe->qhe", dscores, key_one) * scale).astype(jnp.bfloat16)
        key_grad = jnp.einsum("hqk,qhe->khe", dscores, query_wide) * scale
        value_grad = jnp.einsum("hqk,qhe->khe", weights_low, grad_wide)
        key_total = key_total.at[chosen].add(key_grad.reshape(slot_count, TILE, model_width))
        value_total = value_total.at[chosen].add(value_grad.reshape(slot_count, TILE, model_width))
        return (key_total, value_total), (attended.reshape(TILE, model_width), query_grad.reshape(TILE, model_width))

    empty_total = jnp.zeros((NBLK, TILE, model_width), jnp.float32)
    (key_total, value_total), (attended, query_grad) = lax.scan(
        one_tile, (empty_total, empty_total), (query_tiles, grad_tiles, block_lists, tile_lengths))
    return (attended.reshape(FACTS, model_width),
            query_grad.reshape(FACTS, model_width),
            key_total.reshape(DROWS, model_width).astype(jnp.bfloat16),
            value_total.reshape(DROWS, model_width).astype(jnp.bfloat16))
```

```python
import functools

import jax
import jax.numpy as jnp
from jax import lax
from jax.experimental import pallas as pl
from jax.experimental.pallas import tpu as pltpu
from jax.sharding import Mesh, PartitionSpec as P

HEADS = 16
HEAD_DIM = 64
TILE = 128
LANES = 2 * HEAD_DIM
META_ROWS = 16
LOG2E = 1.4426950408889634
SCALE = HEAD_DIM ** (-0.5)
VMEM_LIMIT = 56 * 1024 * 1024


def low_lanes(shape):
    return lax.broadcasted_iota(jnp.int32, shape, len(shape) - 1) < HEAD_DIM


def swap_halves(x):
    return jnp.concatenate([x[:, HEAD_DIM:], x[:, :HEAD_DIM]], axis=1)


def interleave(first, second):
    low = low_lanes(first.shape)
    swapped = swap_halves(second)
    return jnp.where(low, first, swapped), jnp.where(low, swapped, first)


def separate(even, odd):
    low = low_lanes(even.shape)
    return jnp.where(low, even, odd), swap_halves(jnp.where(low, odd, even))


def pack_dimension_kernel(pairs, place, *refs):
    keys, values, outs = refs[:pairs], refs[pairs : 2 * pairs], refs[2 * pairs :]
    odd = (place[2] & 1) == 1
    for i in range(pairs):
        a, b = interleave(keys[i][...], values[i][...])

        @pl.when(odd)
        def _():
            outs[2 * i][...] = b
            outs[2 * i + 1][...] = a

        @pl.when(jnp.logical_not(odd))
        def _():
            outs[2 * i][...] = a
            outs[2 * i + 1][...] = b


def pack_dimension(place, key_rows, value_rows, per_fact):
    rows = key_rows.shape[0]
    pairs = per_fact // 2

    def spec(i):
        return pl.BlockSpec((rows, LANES), lambda _, p: (0, p[0] * pairs + ((p[2] >> 1) ^ i)))

    return pl.pallas_call(
        functools.partial(pack_dimension_kernel, pairs),
        grid_spec=pltpu.PrefetchScalarGridSpec(
            num_scalar_prefetch=1,
            grid=(1,),
            in_specs=[spec(i) for i in range(pairs)] * 2,
            out_specs=[pl.BlockSpec((rows, LANES), lambda _, p: (0, 0))] * per_fact,
        ),
        out_shape=[jax.ShapeDtypeStruct((rows, LANES), jnp.bfloat16)] * per_fact,
        compiler_params=pltpu.CompilerParams(vmem_limit_bytes=VMEM_LIMIT),
        name="pack_dimension",
    )(place, *([key_rows] * pairs), *([value_rows] * pairs))


def pack_fact_kernel(queries, cotangent, meta, out):
    rows = queries.shape[0]
    for p in range(HEADS // 2):
        span = slice(p * LANES, (p + 1) * LANES)
        a, b = interleave(queries[:, span], cotangent[:, span])
        out[2 * p, :rows, :] = a
        out[2 * p + 1, :rows, :] = b
        out[2 * p, rows:, :] = meta[...]
        out[2 * p + 1, rows:, :] = meta[...]


def pack_fact(queries, cotangent, meta):
    rows = queries.shape[0]
    return pl.pallas_call(
        pack_fact_kernel,
        out_shape=jax.ShapeDtypeStruct((HEADS, rows + META_ROWS, LANES), jnp.bfloat16),
        compiler_params=pltpu.CompilerParams(vmem_limit_bytes=VMEM_LIMIT),
        name="pack_fact",
    )(queries, cotangent, meta)


def attend_kernel(owners, slots, place, *refs):
    facts = refs[0]
    tables = refs[1 : 1 + owners]
    fact_out = refs[1 + owners]
    grad_outs = refs[2 + owners : 2 + 2 * owners]
    table, total, meta_words, meta, copy_sems, meta_sem = refs[2 + 2 * owners :]
    sources = facts.shape[0]
    rows = facts.shape[1] - META_ROWS
    tiles_each = rows // TILE
    owner_rows = table.shape[0] // owners
    blocks_each = owner_rows // TILE
    copies = [
        pltpu.make_async_copy(
            tables[i], table.at[pl.ds(i * owner_rows, owner_rows), :], copy_sems.at[i]
        )
        for i in range(owners)
    ]
    for copy in copies:
        copy.start()
    meta_words[...] = facts[:, rows:, :].astype(jnp.float32).astype(jnp.int32)
    meta_copy = pltpu.make_async_copy(meta_words, meta, meta_sem)
    meta_copy.start()
    total[...] = jnp.zeros_like(total)
    meta_copy.wait()
    for copy in copies:
        copy.wait()
    odd = place[2] & 1
    flip = place[1] * blocks_each
    lane = lax.broadcasted_iota(jnp.int32, (TILE, LANES), 1)
    first = (lane // HEAD_DIM) == odd

    def tile_step(index, carry):
        source = index // tiles_each
        tile = index % tiles_each
        length = meta[source, tile, slots]
        start = pl.multiple_of(tile * TILE, TILE)

        def attend(count):
            both = facts[source, pl.ds(start, TILE), :]
            zero = jnp.zeros_like(both)
            left = jnp.concatenate(
                [jnp.where(first, both, zero), jnp.where(first, zero, both)], axis=0
            )
            places = [
                pl.multiple_of((meta[source, tile, j] ^ flip) * TILE, TILE) for j in range(count)
            ]
            kv = jnp.concatenate([table[pl.ds(at, TILE), :] for at in places], axis=0)
            products = lax.dot_general(
                kv, left, (((1,), (1,)), ((), ())), preferred_element_type=jnp.float32
            )
            scores = products[:, :TILE] * (SCALE * LOG2E)
            dweights = products[:, TILE:]
            terms = jnp.exp2(scores - jnp.max(scores, axis=0, keepdims=True))
            weights = terms * (1.0 / jnp.sum(terms, axis=0, keepdims=True))
            row_delta = jnp.sum(weights * dweights, axis=0, keepdims=True)
            dscores = weights * (dweights - row_delta)
            pair = jnp.concatenate(
                [dscores.astype(jnp.bfloat16), weights.astype(jnp.bfloat16)], axis=1
            )
            out = lax.dot_general(
                pair, kv, (((0,), (0,)), ((), ())), preferred_element_type=jnp.float32
            )
            fact_out[source, pl.ds(start, TILE), :] = jnp.where(
                first, out[:TILE] * SCALE, out[TILE:]
            ).astype(jnp.bfloat16)
            grads = jnp.dot(pair, left, preferred_element_type=jnp.float32)
            for j, at in enumerate(places):
                total[pl.ds(at, TILE), :] += grads[j * TILE : (j + 1) * TILE]

        for count in range(1, slots + 1):
            pl.when(length == count)(functools.partial(attend, count))
        return carry

    lax.fori_loop(0, sources * tiles_each, tile_step, 0)
    wide = lax.broadcasted_iota(jnp.int32, (owner_rows, LANES), 1)
    factor = jnp.where((wide // HEAD_DIM) == odd, SCALE, 1.0)
    for i in range(owners):
        grad_outs[i][...] = (
            total[i * owner_rows : (i + 1) * owner_rows, :] * factor
        ).astype(jnp.bfloat16)


def attend(place, facts, tables, slots):
    owners = len(tables)
    owner_rows = tables[0].shape[0]
    sources, rows, _ = facts.shape
    rows -= META_ROWS
    whole = pl.BlockSpec(memory_space=pltpu.VMEM)
    results = pl.pallas_call(
        functools.partial(attend_kernel, owners, slots),
        in_specs=[pl.BlockSpec(memory_space=pltpu.SMEM), whole]
        + [pl.BlockSpec(memory_space=pl.ANY)] * owners,
        out_specs=[whole] * (1 + owners),
        out_shape=[jax.ShapeDtypeStruct((sources, rows, LANES), jnp.bfloat16)]
        + [jax.ShapeDtypeStruct((owner_rows, LANES), jnp.bfloat16)] * owners,
        scratch_shapes=[
            pltpu.VMEM((owners * owner_rows, LANES), jnp.bfloat16),
            pltpu.VMEM((owners * owner_rows, LANES), jnp.float32),
            pltpu.VMEM((sources, META_ROWS, LANES), jnp.int32),
            pltpu.SMEM((sources, META_ROWS, LANES), jnp.int32),
            pltpu.SemaphoreType.DMA((owners,)),
            pltpu.SemaphoreType.DMA,
        ],
        compiler_params=pltpu.CompilerParams(vmem_limit_bytes=VMEM_LIMIT),
        name="attend",
    )(place, facts, *tables)
    return results[0], results[1:]


def unpack_fact_kernel(parts, attended, query_grad):
    for p in range(HEADS // 2):
        span = slice(p * LANES, (p + 1) * LANES)
        query_grad[:, span], attended[:, span] = separate(parts[2 * p], parts[2 * p + 1])


def unpack_fact(parts):
    rows = parts.shape[1]
    shape = jax.ShapeDtypeStruct((rows, HEADS * HEAD_DIM), jnp.bfloat16)
    return pl.pallas_call(
        unpack_fact_kernel,
        out_shape=[shape, shape],
        compiler_params=pltpu.CompilerParams(vmem_limit_bytes=VMEM_LIMIT),
        name="unpack_fact",
    )(parts)


def unpack_dimension_kernel(halves, per_fact, place, *refs):
    parts = refs[: halves * per_fact]
    key_grad, value_grad = refs[halves * per_fact :]
    odd = (place[2] & 1) == 1
    high = place[2] >> 1
    for i in range(per_fact // 2):
        sums = []
        for s in range(2):
            terms = [parts[a * per_fact + 2 * i + s][...].astype(jnp.float32) for a in range(halves)]
            sums.append(functools.reduce(jnp.add, terms).astype(jnp.bfloat16))
        even = jnp.where(odd, sums[1], sums[0])
        uneven = jnp.where(odd, sums[0], sums[1])
        keys, values = separate(even, uneven)
        at = pl.ds(pl.multiple_of((high ^ i) * LANES, LANES), LANES)
        key_grad[:, at] = keys
        value_grad[:, at] = values


def unpack_dimension(place, parts, halves, per_fact):
    rows = parts[0].shape[0]
    shape = jax.ShapeDtypeStruct((rows, per_fact * HEAD_DIM), jnp.bfloat16)
    whole = pl.BlockSpec(memory_space=pltpu.VMEM)
    return pl.pallas_call(
        functools.partial(unpack_dimension_kernel, halves, per_fact),
        in_specs=[pl.BlockSpec(memory_space=pltpu.SMEM)] + [whole] * len(parts),
        out_specs=[whole, whole],
        out_shape=[shape, shape],
        compiler_params=pltpu.CompilerParams(vmem_limit_bytes=VMEM_LIMIT),
        name="unpack_dimension",
    )(place, *parts)


def exchange(parts, halves, per_fact):
    moved = []
    for index, part in enumerate(parts):
        if index == 0:
            moved.append(part)
            continue
        count = halves * per_fact
        moved.append(lax.ppermute(part, ("half", "head"), [(i, i ^ index) for i in range(count)]))
    return moved


def body(halves, per_fact, queries, key_rows, value_rows, cotangent, block_lists, tile_lengths):
    tiles, slots = block_lists.shape
    half, head = lax.axis_index("half"), lax.axis_index("head")
    place = jnp.stack([lax.axis_index("fact"), half * per_fact + head, head]).astype(jnp.int32)
    words = jnp.concatenate([block_lists, tile_lengths[:, None]], axis=1).astype(jnp.bfloat16)
    meta = jnp.pad(words, ((0, META_ROWS - tiles), (0, LANES - slots - 1)))
    packed = pack_dimension(place, key_rows, value_rows, per_fact)
    tables = exchange(list(packed) * halves, halves, per_fact)
    facts = lax.all_to_all(
        pack_fact(queries, cotangent, meta), ("fact", "head"), split_axis=0, concat_axis=0, tiled=True
    )
    fact_out, grads = attend(place, facts, tables, slots)
    grads = exchange(list(grads), halves, per_fact)
    fact_out = lax.all_to_all(fact_out, ("fact", "head"), split_axis=0, concat_axis=0, tiled=True)
    attended, query_grad = unpack_fact(fact_out)
    key_grad, value_grad = unpack_dimension(place, grads, halves, per_fact)
    return attended, query_grad, key_grad, value_grad


def solution(mesh):
    facts, dims = mesh.shape["fact"], mesh.shape["dim"]
    per_fact = HEADS // facts
    halves = dims // per_fact
    fine = Mesh(mesh.devices.reshape(facts, halves, per_fact), ("fact", "half", "head"))
    every = ("fact", "half", "head")
    owner = ("half", "head")
    in_specs = (
        P(every, None),
        P(owner, None),
        P(owner, None),
        P(every, None),
        P(every, None),
        P(every),
    )
    out_specs = (
        P(every, None),
        P(every, None),
        P(owner, "fact"),
        P(owner, "fact"),
    )
    return jax.shard_map(
        functools.partial(body, halves, per_fact),
        mesh=fine,
        in_specs=in_specs,
        out_specs=out_specs,
        check_vma=False,
    )
```

```python
import functools

import jax
import jax.numpy as jnp
from jax import lax
from jax.experimental import pallas as pl
from jax.experimental.pallas import tpu as pltpu
from jax.sharding import Mesh, PartitionSpec as P

HEADS = 16
HEAD_DIM = 64
TILE = 128
LANES = 2 * HEAD_DIM
META_ROWS = 16
LOG2E = 1.4426950408889634
SCALE = HEAD_DIM ** (-0.5)
NEG_FILL = -1e30
PEAK = 1.15e9
MIB = 1024 * 1024
ATTEND_COST = 20
SPLIT_COST = 2
STACK_COST = 2
UNPACK_COST = 3

SMEM = pl.BlockSpec(memory_space=pltpu.SMEM)
VMEM = pl.BlockSpec(memory_space=pltpu.VMEM)


def call(kernel, name, out_shape, in_specs, *, cost, vmem=24, **more):
    return pl.pallas_call(
        kernel,
        out_shape=out_shape,
        in_specs=in_specs,
        out_specs=jax.tree.map(lambda _: VMEM, out_shape),
        compiler_params=pltpu.CompilerParams(vmem_limit_bytes=vmem * MIB),
        cost_estimate=pl.CostEstimate(
            flops=int(cost * PEAK), bytes_accessed=0, transcendentals=0
        ),
        name=name,
        **more,
    )


def bf16(*shape):
    return jax.ShapeDtypeStruct(shape, jnp.bfloat16)


def low_lanes(shape):
    return lax.broadcasted_iota(jnp.int32, shape, len(shape) - 1) < HEAD_DIM


def swap_halves(x):
    return jnp.concatenate([x[:, HEAD_DIM:], x[:, :HEAD_DIM]], axis=1)


def interleave(first, second):
    low = low_lanes(first.shape)
    swapped = swap_halves(second)
    return jnp.where(low, first, swapped), jnp.where(low, swapped, first)


def separate(even, odd):
    low = low_lanes(even.shape)
    return jnp.where(low, even, odd), swap_halves(jnp.where(low, odd, even))


def lane_is(shape, odd):
    return (lax.broadcasted_iota(jnp.int32, shape, len(shape) - 1) // HEAD_DIM) == odd


def in_order(odd, pair):
    a, b = pair
    return jnp.where(odd, b, a), jnp.where(odd, a, b)


def pair_lanes(base, place, i):
    return pl.ds(pl.multiple_of((base + ((place[2] >> 1) ^ i)) * LANES, LANES), LANES)


def pack_dimension(place, key_rows, value_rows, dims, shares):
    rows = key_rows.shape[0] // shares
    pairs = dims // 2

    def kernel(place, *refs):
        keys, values, outs = refs[:pairs], refs[pairs : 2 * pairs], refs[2 * pairs :]
        odd = (place[2] & 1) == 1
        for i in range(pairs):
            outs[2 * i][...], outs[2 * i + 1][...] = in_order(
                odd, interleave(keys[i][...], values[i][...])
            )

    def spec(i):
        return pl.BlockSpec((rows, LANES), lambda _, p: (p[1], p[0] * pairs + ((p[2] >> 1) ^ i)))

    return pl.pallas_call(
        kernel,
        grid_spec=pltpu.PrefetchScalarGridSpec(
            num_scalar_prefetch=1,
            grid=(1,),
            in_specs=[spec(i) for i in range(pairs)] * 2,
            out_specs=[pl.BlockSpec((rows, LANES), lambda _, p: (0, 0))] * dims,
        ),
        out_shape=[bf16(rows, LANES)] * dims,
        compiler_params=pltpu.CompilerParams(vmem_limit_bytes=24 * MIB),
        name="pack_dimension",
    )(place, *([key_rows] * pairs), *([value_rows] * pairs))


def pack_fact(place, queries, cotangent, block_lists, tile_lengths, dims):
    rows = queries.shape[0]
    tiles, slots = block_lists.shape
    parts = HEADS // dims

    def kernel(place, queries, cotangent, block_lists, tile_lengths, *outs):
        odd = (place[2] & 1) == 1
        row = lax.broadcasted_iota(jnp.int32, (META_ROWS, LANES), 0)
        lane = lax.broadcasted_iota(jnp.int32, (META_ROWS, LANES), 1)
        words = jnp.zeros((META_ROWS, LANES), jnp.int32)
        for t in range(tiles):
            for j in range(slots):
                words = jnp.where((row == t) & (lane == j), block_lists[t, j], words)
            words = jnp.where((row == t) & (lane == slots), tile_lengths[t], words)
        meta = words.astype(jnp.float32).astype(jnp.bfloat16)
        for k in range(parts):
            base = (place[0] ^ k) * (dims // 2)
            for i in range(dims // 2):
                span = pair_lanes(base, place, i)
                pair = in_order(odd, interleave(queries[:, span], cotangent[:, span]))
                for s in range(2):
                    outs[k][2 * i + s, :rows, :] = pair[s]
                    outs[k][2 * i + s, rows:, :] = meta

    return call(
        kernel,
        "pack_fact",
        [bf16(dims, rows + META_ROWS, LANES)] * parts,
        [SMEM, VMEM, VMEM, SMEM, SMEM],
        cost=4,
    )(place, queries, cotangent, block_lists, tile_lengths)


def merge_fact(parts):
    dims, rows, _ = parts[0].shape

    def kernel(*refs):
        for r in range(dims):
            for k in range(len(parts)):
                refs[len(parts) + r][k] = refs[k][r]

    return call(
        kernel, "merge_fact", [bf16(len(parts), rows, LANES)] * dims, [VMEM] * len(parts), cost=2
    )(*parts)


def stack_chunks(chunks, cost):
    rows = chunks[0].shape[0]

    def kernel(*refs):
        for r in range(len(chunks)):
            refs[-1][r * rows : (r + 1) * rows, :] = refs[r][...]

    return call(
        kernel, "stack_chunks", bf16(len(chunks) * rows, LANES), [VMEM] * len(chunks), cost=cost
    )(*chunks)


def attend(place, facts, tables, rows, slots):
    dims, shares = len(facts), len(tables)
    parts = facts[0].shape[0]
    sources = dims * parts
    table_rows = tables[0].shape[0]
    owner_blocks = table_rows // TILE // dims
    tiles_each = rows // TILE

    def kernel(place, *refs):
        facts_in, tables_in = refs[:dims], refs[dims : dims + shares]
        fact_outs = refs[dims + shares : 2 * dims + shares]
        own_out = refs[2 * dims + shares]
        share_outs = refs[2 * dims + shares + 1 : 2 * dims + 2 * shares]
        fact, fact_out, table, total, words, meta, sem = refs[2 * dims + 2 * shares :]
        odd = place[2] & 1
        for r in range(dims):
            words[r * parts : (r + 1) * parts] = (
                facts_in[r][:, rows:, :].astype(jnp.float32).astype(jnp.int32)
            )
        copy = pltpu.make_async_copy(words, meta, sem)
        copy.start()
        for r in range(dims):
            fact[r * parts : (r + 1) * parts] = facts_in[r][:, :rows, :]
        for k in range(shares):
            table[k * table_rows : (k + 1) * table_rows, :] = tables_in[k][...]
        total[...] = jnp.zeros_like(total)
        copy.wait()
        first = lane_is((TILE, LANES), odd)

        def row_of(block):
            owner, place_in = block // (shares * owner_blocks), block % (shares * owner_blocks)
            share, at = place_in // owner_blocks, place_in % owner_blocks
            index = ((share ^ place[1]) * dims + (owner ^ place[2])) * owner_blocks + at
            return pl.multiple_of(index * TILE, TILE)

        def step(source, lengths, count):
            left, places, kept, pairs = [], [], [], []
            for tile in range(tiles_each):
                both = fact[source, tile * TILE : (tile + 1) * TILE, :]
                zero = jnp.zeros_like(both)
                left.append(
                    jnp.concatenate(
                        [jnp.where(first, both, zero), jnp.where(first, zero, both)], axis=0
                    )
                )
                places.append([row_of(meta[source, tile, j]) for j in range(count)])
            for tile in range(tiles_each):
                kv = jnp.concatenate([table[pl.ds(at, TILE), :] for at in places[tile]], axis=0)
                products = lax.dot_general(
                    kv, left[tile], (((1,), (1,)), ((), ())), preferred_element_type=jnp.float32
                )
                scores = products[:, :TILE] * (SCALE * LOG2E)
                live = [scores[:TILE]] + [
                    jnp.where(lengths[tile] > j, scores[j * TILE : (j + 1) * TILE], NEG_FILL)
                    for j in range(1, count)
                ]
                scores = jnp.concatenate(live, axis=0)
                dweights = products[:, TILE:]
                terms = jnp.exp2(scores - jnp.max(scores, axis=0, keepdims=True))
                weights = terms * (1.0 / jnp.sum(terms, axis=0, keepdims=True))
                row_delta = jnp.sum(weights * dweights, axis=0, keepdims=True)
                dscores = weights * (dweights - row_delta)
                kept.append(kv)
                pairs.append(
                    jnp.concatenate(
                        [dscores.astype(jnp.bfloat16), weights.astype(jnp.bfloat16)], axis=1
                    )
                )
            for tile in range(tiles_each):
                out = lax.dot_general(
                    pairs[tile],
                    kept[tile],
                    (((0,), (0,)), ((), ())),
                    preferred_element_type=jnp.float32,
                )
                fact_out[source, tile * TILE : (tile + 1) * TILE, :] = jnp.where(
                    first, out[:TILE] * SCALE, out[TILE:]
                ).astype(jnp.bfloat16)
                grads = jnp.dot(pairs[tile], left[tile], preferred_element_type=jnp.float32)
                for j, at in enumerate(places[tile]):
                    total[pl.ds(at, TILE), :] += grads[j * TILE : (j + 1) * TILE]

        def source_step(source, carry):
            lengths = [meta[source, tile, slots] for tile in range(tiles_each)]
            longest = functools.reduce(jnp.maximum, lengths)
            for count in range(1, slots + 1):
                pl.when(longest == count)(functools.partial(step, source, lengths, count))
            return carry

        lax.fori_loop(0, sources, source_step, 0)
        for r in range(dims):
            fact_outs[r][...] = fact_out[r * parts : (r + 1) * parts]
        factor = jnp.where(lane_is((table_rows, LANES), odd), SCALE, 1.0)
        own_out[...] = total[:table_rows] * factor
        for k in range(1, shares):
            share_outs[k - 1][...] = (
                total[k * table_rows : (k + 1) * table_rows] * factor
            ).astype(jnp.bfloat16)

    results = call(
        kernel,
        "attend",
        [bf16(parts, rows, LANES)] * dims
        + [jax.ShapeDtypeStruct((table_rows, LANES), jnp.float32)]
        + [bf16(table_rows, LANES)] * (shares - 1),
        [SMEM] + [VMEM] * (dims + shares),
        cost=ATTEND_COST,
        vmem=40,
        scratch_shapes=[
            pltpu.VMEM((sources, rows, LANES), jnp.bfloat16),
            pltpu.VMEM((sources, rows, LANES), jnp.bfloat16),
            pltpu.VMEM((shares * table_rows, LANES), jnp.bfloat16),
            pltpu.VMEM((shares * table_rows, LANES), jnp.float32),
            pltpu.VMEM((sources, META_ROWS, LANES), jnp.int32),
            pltpu.SMEM((sources, META_ROWS, LANES), jnp.int32),
            pltpu.SemaphoreType.DMA,
        ],
    )(place, *facts, *tables)
    return results[:dims], results[dims], results[dims + 1 :]


def split_fact(chunks):
    parts, rows, _ = chunks[0].shape
    dims = len(chunks)

    def kernel(*refs):
        for k in range(parts):
            for r in range(dims):
                refs[dims + k][r] = refs[r][k]

    return call(
        kernel, "split_fact", [bf16(dims, rows, LANES)] * parts, [VMEM] * dims, cost=SPLIT_COST
    )(*chunks)


def unpack_fact(place, parts):
    dims, rows, _ = parts[0].shape

    def kernel(place, *refs):
        attended, query_grad = refs[len(parts) :]
        odd = (place[2] & 1) == 1
        for k in range(len(parts)):
            base = (place[0] ^ k) * (dims // 2)
            for i in range(dims // 2):
                span = pair_lanes(base, place, i)
                pair = in_order(odd, (refs[k][2 * i], refs[k][2 * i + 1]))
                query_grad[:, span], attended[:, span] = separate(*pair)

    return call(
        kernel,
        "unpack_fact",
        [bf16(rows, HEADS * HEAD_DIM)] * 2,
        [SMEM] + [VMEM] * len(parts),
        cost=2.4,
    )(place, *parts)


def sum_shares(place, own, others, dims, per_fact):
    rows = own.shape[0] // dims

    def kernel(place, own, *refs):
        others_in, outs = refs[: len(others)], refs[len(others) :]
        for r in range(dims):
            at = pl.multiple_of((r ^ (place[1] * per_fact)) * rows, rows)
            total = own[pl.ds(at, rows), :]
            for other in others_in:
                total += other[pl.ds(at, rows), :].astype(jnp.float32)
            outs[r][...] = total.astype(jnp.bfloat16)

    return call(
        kernel, "sum_shares", [bf16(rows, LANES)] * dims, [SMEM] + [VMEM] * (1 + len(others)), cost=2
    )(place, own, *others)


def unpack_dimension(place, chunks, shares, per_fact):
    dims = len(chunks)
    rows = chunks[0].shape[0]

    def kernel(place, *refs):
        key_grad, value_grad = refs[dims:]
        odd = (place[2] & 1) == 1
        for i in range(dims // 2):
            source = place[2] ^ (2 * i)
            share = (source // per_fact) ^ place[1]
            pair = in_order(odd, (refs[2 * i][...], refs[2 * i + 1][...]))
            at = pl.ds(pl.multiple_of(share * rows, rows), rows)
            span = pl.ds(pl.multiple_of(((source % per_fact) // 2) * LANES, LANES), LANES)
            key_grad[at, span], value_grad[at, span] = separate(*pair)

    return call(
        kernel,
        "unpack_dimension",
        [bf16(shares * rows, per_fact * HEAD_DIM)] * 2,
        [SMEM] + [VMEM] * dims,
        cost=UNPACK_COST,
    )(place, *chunks)


def by_xor(part, axis, index, count):
    if index == 0:
        return part
    return lax.ppermute(part, axis, [(i, i ^ index) for i in range(count)])


def body(xs, shares, dims, queries, key_rows, value_rows, cotangent, block_lists, tile_lengths):
    per_fact = dims // shares
    rows, slots = queries.shape[0], block_lists.shape[1]
    place = jnp.stack([lax.axis_index(a) for a in ("x", "share", "dim")]).astype(jnp.int32)

    chunks = pack_dimension(place, key_rows, value_rows, dims, shares)
    chunks = [by_xor(chunk, "dim", r, dims) for r, chunk in enumerate(chunks)]
    table = stack_chunks(chunks, STACK_COST)
    tables = [by_xor(table, "share", k, shares) for k in range(shares)]

    parts = pack_fact(place, queries, cotangent, block_lists, tile_lengths, dims)
    parts = [by_xor(part, "x", k, xs) for k, part in enumerate(parts)]
    facts = merge_fact(parts)
    facts = [by_xor(chunk, "dim", r, dims) for r, chunk in enumerate(facts)]

    fact_outs, own, others = attend(place, facts, tables, rows, slots)

    fact_outs = [by_xor(chunk, "dim", r, dims) for r, chunk in enumerate(fact_outs)]
    parts = split_fact(fact_outs)
    parts = [by_xor(part, "x", k, xs) for k, part in enumerate(parts)]
    attended, query_grad = unpack_fact(place, parts)

    others = [by_xor(other, "share", k + 1, shares) for k, other in enumerate(others)]
    chunks = sum_shares(place, own, others, dims, per_fact)
    grads = []
    for r, chunk in enumerate(chunks):
        pairs = [
            (c * dims + d, (d // per_fact) * dims + (d ^ r ^ (c * per_fact)))
            for c in range(shares)
            for d in range(dims)
        ]
        grads.append(lax.ppermute(chunk, ("share", "dim"), pairs))
    key_grad, value_grad = unpack_dimension(place, grads, shares, per_fact)
    return attended, query_grad, key_grad, value_grad


def solution(mesh):
    facts, dims = mesh.shape["fact"], mesh.shape["dim"]
    xs = HEADS // dims
    shares = facts // xs
    fine = Mesh(mesh.devices.reshape(xs, shares, dims), ("x", "share", "dim"))
    every = ("x", "share", "dim")
    in_specs = (
        P(every, None),
        P("dim", None),
        P("dim", None),
        P(every, None),
        P(every, None),
        P(every),
    )
    out_specs = (
        P(every, None),
        P(every, None),
        P("dim", ("x", "share")),
        P("dim", ("x", "share")),
    )
    return jax.shard_map(
        functools.partial(body, xs, shares, dims),
        mesh=fine,
        in_specs=in_specs,
        out_specs=out_specs,
        check_vma=False,
    )
```

```python
import functools

import jax
import jax.numpy as jnp
from jax import lax
from jax.experimental import pallas as pl
from jax.experimental.pallas import tpu as pltpu
from jax.sharding import Mesh, PartitionSpec as P

HEADS = 16
HEAD_DIM = 64
TILE = 128
LANES = 2 * HEAD_DIM
META_ROWS = 16
LOG2E = 1.4426950408889634
SCALE = HEAD_DIM ** (-0.5)
NEG_FILL = -1e30
PEAK = 1.15e9
MIB = 1024 * 1024
BATCHES = ((0, 4, 0), (4, 8, 0))
SPLIT_COST = 0
UNPACK_FACT = 2
PLANES = 4
STACK_COST = 2
UNPACK_COST = 5

SMEM = pl.BlockSpec(memory_space=pltpu.SMEM)
VMEM = pl.BlockSpec(memory_space=pltpu.VMEM)


def call(kernel, name, out_shape, in_specs, *, cost, vmem=24, **more):
    return pl.pallas_call(
        kernel,
        out_shape=out_shape,
        in_specs=in_specs,
        out_specs=jax.tree.map(lambda _: VMEM, out_shape),
        compiler_params=pltpu.CompilerParams(vmem_limit_bytes=vmem * MIB),
        cost_estimate=pl.CostEstimate(
            flops=int(cost * PEAK), bytes_accessed=0, transcendentals=0
        ),
        name=name,
        **more,
    )


def bf16(*shape):
    return jax.ShapeDtypeStruct(shape, jnp.bfloat16)


def low_lanes(shape):
    return lax.broadcasted_iota(jnp.int32, shape, len(shape) - 1) < HEAD_DIM


def swap_halves(x):
    return jnp.concatenate([x[:, HEAD_DIM:], x[:, :HEAD_DIM]], axis=1)


def interleave(first, second):
    low = low_lanes(first.shape)
    swapped = swap_halves(second)
    return jnp.where(low, first, swapped), jnp.where(low, swapped, first)


def separate(even, odd):
    low = low_lanes(even.shape)
    return jnp.where(low, even, odd), swap_halves(jnp.where(low, odd, even))


def lane_is(shape, odd):
    return (lax.broadcasted_iota(jnp.int32, shape, len(shape) - 1) // HEAD_DIM) == odd


def in_order(odd, pair):
    a, b = pair
    return jnp.where(odd, b, a), jnp.where(odd, a, b)


def pair_lanes(base, place, i):
    return pl.ds(pl.multiple_of((base + ((place[2] >> 1) ^ i)) * LANES, LANES), LANES)


def pack_dimension(place, key_rows, value_rows, dims, shares):
    rows = key_rows.shape[0] // shares
    pairs = dims // 2

    def kernel(place, *refs):
        keys, values, outs = refs[:pairs], refs[pairs : 2 * pairs], refs[2 * pairs :]
        odd = (place[2] & 1) == 1
        for i in range(pairs):
            outs[2 * i][...], outs[2 * i + 1][...] = in_order(
                odd, interleave(keys[i][...], values[i][...])
            )

    def spec(i):
        return pl.BlockSpec((rows, LANES), lambda _, p: (p[1], p[0] * pairs + ((p[2] >> 1) ^ i)))

    return pl.pallas_call(
        kernel,
        grid_spec=pltpu.PrefetchScalarGridSpec(
            num_scalar_prefetch=1,
            grid=(1,),
            in_specs=[spec(i) for i in range(pairs)] * 2,
            out_specs=[pl.BlockSpec((rows, LANES), lambda _, p: (0, 0))] * dims,
        ),
        out_shape=[bf16(rows, LANES)] * dims,
        compiler_params=pltpu.CompilerParams(vmem_limit_bytes=60 * MIB),
        name="pack_dimension",
    )(place, *([key_rows] * pairs), *([value_rows] * pairs))


def pack_fact(place, queries, cotangent, block_lists, tile_lengths, dims):
    rows = queries.shape[0]
    tiles, slots = block_lists.shape
    parts = HEADS // dims

    def kernel(place, queries, cotangent, block_lists, tile_lengths, *refs):
        *outs, words = refs
        odd = (place[2] & 1) == 1
        words[...] = jnp.zeros_like(words)
        words[:tiles, :slots] = block_lists[...]
        words[:tiles, slots : slots + 1] = tile_lengths[...]
        meta = words[...].astype(jnp.float32).astype(jnp.bfloat16)
        for k in range(parts):
            base = (place[0] ^ k) * (dims // 2)
            for i in range(dims // 2):
                span = pair_lanes(base, place, i)
                pair = in_order(odd, interleave(queries[:, span], cotangent[:, span]))
                for s in range(2):
                    outs[k][2 * i + s, :rows, :] = pair[s]
                    outs[k][2 * i + s, rows:, :] = meta

    return call(
        kernel,
        "pack_fact",
        [bf16(dims, rows + META_ROWS, LANES)] * parts,
        [SMEM, VMEM, VMEM, VMEM, VMEM],
        cost=1,
        scratch_shapes=[pltpu.VMEM((META_ROWS, LANES), jnp.int32)],
    )(place, queries, cotangent, block_lists, tile_lengths[:, None])


def merge_fact(parts):
    dims, rows, _ = parts[0].shape

    def kernel(*refs):
        for r in range(dims):
            for k in range(len(parts)):
                refs[len(parts) + r][k] = refs[k][r]

    return call(
        kernel, "merge_fact", [bf16(len(parts), rows, LANES)] * dims, [VMEM] * len(parts), cost=2
    )(*parts)


def stack_chunks(chunks, cost):
    rows = chunks[0].shape[0]

    def kernel(*refs):
        for r, chunk in enumerate(refs[:-1]):
            refs[-1][r * rows : (r + 1) * rows, :] = chunk[...]

    return call(
        kernel, "stack_chunks", bf16(len(chunks) * rows, LANES), [VMEM] * len(chunks), cost=cost
    )(*chunks)


def attend(place, facts, tables, total, rows, slots, dims, shares, ys, last, cost):
    count = len(facts)
    parts = facts[0].shape[0]
    sources = count * parts
    table_rows = sum(t.shape[0] for t in tables) // shares
    owner_blocks = table_rows // TILE // dims
    tiles_each = rows // TILE
    begin = total is None

    def kernel(place, *refs):
        refs = list(refs)

        def take(n):
            taken = refs[:n]
            del refs[:n]
            return taken

        facts_in = take(count)
        tables_in = take(len(tables))
        (total_in,) = take(1) if not begin else (None,)
        fact_outs = take(count // ys)
        if last:
            (own_out,), share_outs = take(1), take(shares - 1)
        else:
            (sums_out,) = take(1)
        (table,) = take(1) if begin else tables_in
        (sums,) = take(1) if last else (sums_out,)
        fact, fact_out, words, meta, sem = refs
        odd = place[2] & 1
        for r in range(count):
            words[r * parts : (r + 1) * parts] = (
                facts_in[r][:, rows:, :].astype(jnp.float32).astype(jnp.int32)
            )
        copy = pltpu.make_async_copy(words, meta, sem)
        copy.start()
        for r in range(count):
            fact[r * parts : (r + 1) * parts] = facts_in[r][:, :rows, :]
        if begin:
            for k in range(shares):
                table[k * table_rows : (k + 1) * table_rows, :] = tables_in[k][...]
            sums[...] = jnp.zeros_like(sums)
        else:
            sums[...] = total_in[...]
        copy.wait()
        first = lane_is((TILE, LANES), odd)

        def row_of(block):
            owner, place_in = block // (shares * owner_blocks), block % (shares * owner_blocks)
            share, at = place_in // owner_blocks, place_in % owner_blocks
            index = ((share ^ place[1]) * dims + (owner ^ place[2])) * owner_blocks + at
            return pl.multiple_of(index * TILE, TILE)

        def step(source, lengths, count):
            left, places, kept, pairs = [], [], [], []
            for tile in range(tiles_each):
                both = fact[source, tile * TILE : (tile + 1) * TILE, :]
                zero = jnp.zeros_like(both)
                left.append(
                    jnp.concatenate(
                        [jnp.where(first, both, zero), jnp.where(first, zero, both)], axis=0
                    )
                )
                places.append([row_of(meta[source, tile, j]) for j in range(count)])
            for tile in range(tiles_each):
                kv = jnp.concatenate([table[pl.ds(at, TILE), :] for at in places[tile]], axis=0)
                products = lax.dot_general(
                    kv, left[tile], (((1,), (1,)), ((), ())), preferred_element_type=jnp.float32
                )
                scores = products[:, :TILE] * (SCALE * LOG2E)
                live = [scores[:TILE]] + [
                    jnp.where(lengths[tile] > j, scores[j * TILE : (j + 1) * TILE], NEG_FILL)
                    for j in range(1, count)
                ]
                scores = jnp.concatenate(live, axis=0)
                dweights = products[:, TILE:]
                terms = jnp.exp2(scores - jnp.max(scores, axis=0, keepdims=True))
                weights = terms * (1.0 / jnp.sum(terms, axis=0, keepdims=True))
                row_delta = jnp.sum(weights * dweights, axis=0, keepdims=True)
                dscores = weights * (dweights - row_delta)
                kept.append(kv)
                pairs.append(
                    jnp.concatenate(
                        [dscores.astype(jnp.bfloat16), weights.astype(jnp.bfloat16)], axis=1
                    )
                )
            for tile in range(tiles_each):
                out = lax.dot_general(
                    pairs[tile],
                    kept[tile],
                    (((0,), (0,)), ((), ())),
                    preferred_element_type=jnp.float32,
                )
                fact_out[source, tile * TILE : (tile + 1) * TILE, :] = jnp.where(
                    first, out[:TILE] * SCALE, out[TILE:]
                ).astype(jnp.bfloat16)
                grads = jnp.dot(pairs[tile], left[tile], preferred_element_type=jnp.float32)
                for j, at in enumerate(places[tile]):
                    sums[pl.ds(at, TILE), :] += grads[j * TILE : (j + 1) * TILE]

        def source_step(source, carry):
            lengths = [meta[source, tile, slots] for tile in range(tiles_each)]
            longest = functools.reduce(jnp.maximum, lengths)
            for count in range(1, slots + 1):
                pl.when(longest == count)(functools.partial(step, source, lengths, count))
            return carry

        lax.fori_loop(0, sources, source_step, 0)
        for r in range(count):
            for i in range(parts):
                fact_outs[r // ys][i * ys + r % ys] = fact_out[r * parts + i]
        if last:
            factor = jnp.where(lane_is((table_rows, LANES), odd), SCALE, 1.0)
            own_out[...] = sums[:table_rows] * factor
            for k in range(1, shares):
                share_outs[k - 1][...] = (
                    sums[k * table_rows : (k + 1) * table_rows] * factor
                ).astype(jnp.bfloat16)

    outs = [bf16(parts * ys, rows, LANES)] * (count // ys)
    wide = jax.ShapeDtypeStruct((shares * table_rows, LANES), jnp.float32)
    scratch = []
    if last:
        outs += [jax.ShapeDtypeStruct((table_rows, LANES), jnp.float32)]
        outs += [bf16(table_rows, LANES)] * (shares - 1)
    else:
        outs += [wide]
    if begin:
        if last:
            scratch += [pltpu.VMEM((shares * table_rows, LANES), jnp.bfloat16)]
        else:
            outs += [bf16(shares * table_rows, LANES)]
    if last:
        scratch += [pltpu.VMEM(wide.shape, wide.dtype)]
    sums_in = [] if begin else [total]
    results = call(
        kernel,
        "attend",
        outs,
        [SMEM] + [VMEM] * (count + len(tables) + len(sums_in)),
        cost=cost,
        vmem=32,
        scratch_shapes=scratch
        + [
            pltpu.VMEM((sources, rows, LANES), jnp.bfloat16),
            pltpu.VMEM((sources, rows, LANES), jnp.bfloat16),
            pltpu.VMEM((sources, META_ROWS, LANES), jnp.int32),
            pltpu.SMEM((sources, META_ROWS, LANES), jnp.int32),
            pltpu.SemaphoreType.DMA,
        ],
    )(place, *facts, *tables, *sums_in)
    return results[: count // ys], results[count // ys :]


def join_planes(place, chunks, xs, cost):
    zs, (count, rows, _) = len(chunks), chunks[0].shape
    ys = count // xs

    def kernel(place, *refs):
        for k in range(zs):
            for n in range(count):
                i, j = divmod(n, ys)
                m = (place[0] ^ i) * ys + (place[4] ^ j)
                refs[zs][m, place[3] ^ k] = refs[zs - 1 - k][n]

    return call(
        kernel, "join_planes", bf16(count, zs, rows, LANES), [SMEM] + [VMEM] * zs, cost=cost
    )(place, *chunks[::-1])


def unpack_fact(parts, xs):
    planes, zs, rows, _ = parts.shape
    ys = planes // xs

    def kernel(parts, attended, query_grad):
        for p in range(HEADS // 2):
            span = slice(p * LANES, (p + 1) * LANES)
            x, dim = divmod(2 * p, zs * ys)
            m, z = x * ys + dim % ys, dim // ys
            query_grad[:, span], attended[:, span] = separate(parts[m, z], parts[m + 1, z])

    return call(
        kernel, "unpack_fact", [bf16(rows, HEADS * HEAD_DIM)] * 2, [VMEM], cost=UNPACK_FACT
    )(parts)


def sum_shares(place, own, others, dims, per_fact):
    rows = own.shape[0] // dims

    def kernel(place, own, *refs):
        others_in, outs = refs[: len(others)], refs[len(others) :]
        for r in range(dims):
            at = pl.multiple_of((r ^ (place[1] * per_fact)) * rows, rows)
            total = own[pl.ds(at, rows), :]
            for other in others_in:
                total += other[pl.ds(at, rows), :].astype(jnp.float32)
            outs[r][...] = total.astype(jnp.bfloat16)

    return call(
        kernel, "sum_shares", [bf16(rows, LANES)] * dims, [SMEM] + [VMEM] * (1 + len(others)), cost=2
    )(place, own, *others)


def unpack_dimension(place, chunks, shares, per_fact):
    dims = len(chunks)
    rows = chunks[0].shape[0]

    def kernel(place, *refs):
        key_grad, value_grad = refs[dims:]
        refs = refs[dims - 1 :: -1]
        odd = (place[2] & 1) == 1
        for i in range(dims // 2):
            source = place[2] ^ (2 * i)
            share = (source // per_fact) ^ place[1]
            pair = in_order(odd, (refs[2 * i][...], refs[2 * i + 1][...]))
            at = pl.ds(pl.multiple_of(share * rows, rows), rows)
            span = pl.ds(pl.multiple_of(((source % per_fact) // 2) * LANES, LANES), LANES)
            key_grad[at, span], value_grad[at, span] = separate(*pair)

    return call(
        kernel,
        "unpack_dimension",
        [bf16(shares * rows, per_fact * HEAD_DIM)] * 2,
        [SMEM] + [VMEM] * dims,
        cost=UNPACK_COST,
    )(place, *reversed(chunks))


def by_xor(part, axis, index, count):
    if index == 0:
        return part
    return lax.ppermute(part, axis, [(i, i ^ index) for i in range(count)])


def exchange(chunks, send):
    moved = list(chunks)
    for r in range(len(chunks)):
        moved[r] = send(chunks[r], r)
    return moved


def body(xs, shares, zs, ys, queries, key_rows, value_rows, cotangent, block_lists, tile_lengths):
    dims = zs * ys
    per_fact = dims // shares
    rows, slots = queries.shape[0], block_lists.shape[1]
    x, share, z, y = (lax.axis_index(a) for a in ("x", "share", "z", "y"))
    place = jnp.stack([x, share, z * ys + y, z, y]).astype(jnp.int32)

    def over_dim(chunk, r):
        return by_xor(chunk, ("z", "y"), r, dims)

    def to_columns(chunk, r):
        pairs = [
            (c * dims + d, (d // per_fact) * dims + (d ^ r ^ (c * per_fact)))
            for c in range(shares)
            for d in range(dims)
        ]
        return lax.ppermute(chunk, ("share", "z", "y"), pairs)

    chunks = pack_dimension(place, key_rows, value_rows, dims, shares)
    chunks = exchange(chunks, over_dim)
    table = stack_chunks(chunks, STACK_COST)
    tables = [by_xor(table, "share", k, shares) for k in range(shares)]

    parts = pack_fact(place, queries, cotangent, block_lists, tile_lengths, dims)
    parts = [by_xor(part, "x", k, xs) for k, part in enumerate(parts)]
    facts = merge_fact(parts)
    facts = exchange(facts, over_dim)

    fact_outs, total = [], None
    for start, stop, cost in BATCHES:
        stop = min(stop * dims // 8, dims)
        outs, rest = attend(
            place,
            facts[start * dims // 8 : stop],
            tables,
            total,
            rows,
            slots,
            dims,
            shares,
            ys,
            stop == dims,
            cost,
        )
        fact_outs += outs
        if stop < dims:
            total = rest[0]
            tables = rest[1:] or tables
    own, others = rest[0], rest[1:]

    fact_outs = [by_xor(chunk, "z", k, zs) for k, chunk in enumerate(fact_outs)]
    others = [by_xor(other, "share", k + 1, shares) for k, other in enumerate(others)]
    chunks = sum_shares(place, own, others, dims, per_fact)
    fact_outs[0], *chunks = lax.optimization_barrier((fact_outs[0], *chunks))
    fact_out = join_planes(place, fact_outs, xs, SPLIT_COST)
    fact_out = lax.all_to_all(fact_out, ("x", "y"), split_axis=0, concat_axis=0, tiled=True)
    attended, query_grad = unpack_fact(fact_out, xs)

    grads = exchange(chunks, to_columns)
    key_grad, value_grad = unpack_dimension(place, grads, shares, per_fact)
    return attended, query_grad, key_grad, value_grad


def solution(mesh):
    facts, dims = mesh.shape["fact"], mesh.shape["dim"]
    xs = HEADS // dims
    shares = facts // xs
    ys = dims // PLANES
    every = ("x", "share", "z", "y")
    fine = Mesh(mesh.devices.reshape(xs, shares, PLANES, ys), every)
    owner, columns = ("z", "y"), ("x", "share")
    in_specs = (
        P(every, None),
        P(owner, None),
        P(owner, None),
        P(every, None),
        P(every, None),
        P(every),
    )
    out_specs = (
        P(every, None),
        P(every, None),
        P(owner, columns),
        P(owner, columns),
    )
    return jax.shard_map(
        functools.partial(body, xs, shares, PLANES, ys),
        mesh=fine,
        in_specs=in_specs,
        out_specs=out_specs,
        check_vma=False,
    )
```

```python
import functools

import jax
import jax.numpy as jnp
from jax import lax
from jax.experimental import pallas as pl
from jax.experimental.pallas import tpu as pltpu
from jax.sharding import Mesh, PartitionSpec as P

HEADS = 16
HEAD_DIM = 64
TILE = 128
LANES = 2 * HEAD_DIM
META_ROWS = 16
LOG2E = 1.4426950408889634
SCALE = HEAD_DIM ** (-0.5)
NEG_FILL = -1e30
PEAK = 1.15e9
MIB = 1024 * 1024
BATCHES = ((0, 4, 0), (4, 6, 0), (6, 8, 60))
SPLIT_COST = 0
UNPACK_FACT = 2
PLANES = 4
STACK_COST = 2
UNPACK_COST = 5

SMEM = pl.BlockSpec(memory_space=pltpu.SMEM)
VMEM = pl.BlockSpec(memory_space=pltpu.VMEM)


def call(kernel, name, out_shape, in_specs, *, cost, vmem=24, **more):
    return pl.pallas_call(
        kernel,
        out_shape=out_shape,
        in_specs=in_specs,
        out_specs=jax.tree.map(lambda _: VMEM, out_shape),
        compiler_params=pltpu.CompilerParams(vmem_limit_bytes=vmem * MIB),
        cost_estimate=pl.CostEstimate(
            flops=int(cost * PEAK), bytes_accessed=0, transcendentals=0
        ),
        name=name,
        **more,
    )


def bf16(*shape):
    return jax.ShapeDtypeStruct(shape, jnp.bfloat16)


def low_lanes(shape):
    return lax.broadcasted_iota(jnp.int32, shape, len(shape) - 1) < HEAD_DIM


def swap_halves(x):
    return jnp.concatenate([x[:, HEAD_DIM:], x[:, :HEAD_DIM]], axis=1)


def interleave(first, second):
    low = low_lanes(first.shape)
    swapped = swap_halves(second)
    return jnp.where(low, first, swapped), jnp.where(low, swapped, first)


def separate(even, odd):
    low = low_lanes(even.shape)
    return jnp.where(low, even, odd), swap_halves(jnp.where(low, odd, even))


def lane_is(shape, odd):
    return (lax.broadcasted_iota(jnp.int32, shape, len(shape) - 1) // HEAD_DIM) == odd


def in_order(odd, pair):
    a, b = pair
    return jnp.where(odd, b, a), jnp.where(odd, a, b)


def pair_lanes(base, place, i):
    return pl.ds(pl.multiple_of((base + ((place[2] >> 1) ^ i)) * LANES, LANES), LANES)


def pack_dimension(place, key_rows, value_rows, dims, shares):
    rows = key_rows.shape[0] // shares
    pairs = dims // 2

    def kernel(place, *refs):
        keys, values, outs = refs[:pairs], refs[pairs : 2 * pairs], refs[2 * pairs :]
        odd = (place[2] & 1) == 1
        for i in range(pairs):
            outs[2 * i][...], outs[2 * i + 1][...] = in_order(
                odd, interleave(keys[i][...], values[i][...])
            )

    def spec(i):
        return pl.BlockSpec((rows, LANES), lambda _, p: (p[1], p[0] * pairs + ((p[2] >> 1) ^ i)))

    return pl.pallas_call(
        kernel,
        grid_spec=pltpu.PrefetchScalarGridSpec(
            num_scalar_prefetch=1,
            grid=(1,),
            in_specs=[spec(i) for i in range(pairs)] * 2,
            out_specs=[pl.BlockSpec((rows, LANES), lambda _, p: (0, 0))] * dims,
        ),
        out_shape=[bf16(rows, LANES)] * dims,
        compiler_params=pltpu.CompilerParams(vmem_limit_bytes=60 * MIB),
        name="pack_dimension",
    )(place, *([key_rows] * pairs), *([value_rows] * pairs))


def pack_fact(place, queries, cotangent, block_lists, tile_lengths, dims):
    rows = queries.shape[0]
    tiles, slots = block_lists.shape
    parts = HEADS // dims

    def kernel(place, queries, cotangent, block_lists, tile_lengths, *refs):
        *outs, words = refs
        odd = (place[2] & 1) == 1
        words[...] = jnp.zeros_like(words)
        words[:tiles, :slots] = block_lists[...]
        words[:tiles, slots : slots + 1] = tile_lengths[...]
        meta = words[...].astype(jnp.float32).astype(jnp.bfloat16)
        for k in range(parts):
            base = (place[0] ^ k) * (dims // 2)
            for i in range(dims // 2):
                span = pair_lanes(base, place, i)
                pair = in_order(odd, interleave(queries[:, span], cotangent[:, span]))
                for s in range(2):
                    outs[k][2 * i + s, :rows, :] = pair[s]
                    outs[k][2 * i + s, rows:, :] = meta

    return call(
        kernel,
        "pack_fact",
        [bf16(dims, rows + META_ROWS, LANES)] * parts,
        [SMEM, VMEM, VMEM, VMEM, VMEM],
        cost=1,
        scratch_shapes=[pltpu.VMEM((META_ROWS, LANES), jnp.int32)],
    )(place, queries, cotangent, block_lists, tile_lengths[:, None])


def merge_fact(parts):
    dims, rows, _ = parts[0].shape

    def kernel(*refs):
        for r in range(dims):
            for k in range(len(parts)):
                refs[len(parts) + r][k] = refs[k][r]

    return call(
        kernel, "merge_fact", [bf16(len(parts), rows, LANES)] * dims, [VMEM] * len(parts), cost=2
    )(*parts)


def stack_chunks(chunks, cost):
    rows = chunks[0].shape[0]

    def kernel(*refs):
        for r, chunk in enumerate(refs[:-1]):
            refs[-1][r * rows : (r + 1) * rows, :] = chunk[...]

    return call(
        kernel, "stack_chunks", bf16(len(chunks) * rows, LANES), [VMEM] * len(chunks), cost=cost
    )(*chunks)


def attend(place, facts, tables, total, rows, slots, dims, shares, ys, last, cost):
    count = len(facts)
    parts = facts[0].shape[0]
    sources = count * parts
    table_rows = sum(t.shape[0] for t in tables) // shares
    owner_blocks = table_rows // TILE // dims
    tiles_each = rows // TILE
    begin = total is None

    def kernel(place, *refs):
        refs = list(refs)

        def take(n):
            taken = refs[:n]
            del refs[:n]
            return taken

        facts_in = take(count)
        tables_in = take(len(tables))
        (total_in,) = take(1) if not begin else (None,)
        fact_outs = take(count // ys)
        if last:
            (own_out,), share_outs = take(1), take(shares - 1)
        else:
            (sums_out,) = take(1)
        (table,) = take(1) if begin else tables_in
        (sums,) = take(1) if last else (sums_out,)
        fact, fact_out, words, meta, sem = refs
        odd = place[2] & 1
        for r in range(count):
            words[r * parts : (r + 1) * parts] = (
                facts_in[r][:, rows:, :].astype(jnp.float32).astype(jnp.int32)
            )
        copy = pltpu.make_async_copy(words, meta, sem)
        copy.start()
        for r in range(count):
            fact[r * parts : (r + 1) * parts] = facts_in[r][:, :rows, :]
        if begin:
            for k in range(shares):
                table[k * table_rows : (k + 1) * table_rows, :] = tables_in[k][...]
            sums[...] = jnp.zeros_like(sums)
        else:
            sums[...] = total_in[...]
        copy.wait()
        first = lane_is((TILE, LANES), odd)

        def row_of(block):
            owner, place_in = block // (shares * owner_blocks), block % (shares * owner_blocks)
            share, at = place_in // owner_blocks, place_in % owner_blocks
            index = ((share ^ place[1]) * dims + (owner ^ place[2])) * owner_blocks + at
            return pl.multiple_of(index * TILE, TILE)

        def step(source, lengths, count):
            left, places, kept, pairs = [], [], [], []
            for tile in range(tiles_each):
                both = fact[source, tile * TILE : (tile + 1) * TILE, :]
                zero = jnp.zeros_like(both)
                left.append(
                    jnp.concatenate(
                        [jnp.where(first, both, zero), jnp.where(first, zero, both)], axis=0
                    )
                )
                places.append([row_of(meta[source, tile, j]) for j in range(count)])
            for tile in range(tiles_each):
                kv = jnp.concatenate([table[pl.ds(at, TILE), :] for at in places[tile]], axis=0)
                products = lax.dot_general(
                    kv, left[tile], (((1,), (1,)), ((), ())), preferred_element_type=jnp.float32
                )
                scores = products[:, :TILE] * (SCALE * LOG2E)
                live = [scores[:TILE]] + [
                    jnp.where(lengths[tile] > j, scores[j * TILE : (j + 1) * TILE], NEG_FILL)
                    for j in range(1, count)
                ]
                scores = jnp.concatenate(live, axis=0)
                dweights = products[:, TILE:]
                terms = jnp.exp2(scores - jnp.max(scores, axis=0, keepdims=True))
                weights = terms * (1.0 / jnp.sum(terms, axis=0, keepdims=True))
                row_delta = jnp.sum(weights * dweights, axis=0, keepdims=True)
                dscores = weights * (dweights - row_delta)
                kept.append(kv)
                pairs.append(
                    jnp.concatenate(
                        [dscores.astype(jnp.bfloat16), weights.astype(jnp.bfloat16)], axis=1
                    )
                )
            for tile in range(tiles_each):
                out = lax.dot_general(
                    pairs[tile],
                    kept[tile],
                    (((0,), (0,)), ((), ())),
                    preferred_element_type=jnp.float32,
                )
                fact_out[source, tile * TILE : (tile + 1) * TILE, :] = jnp.where(
                    first, out[:TILE] * SCALE, out[TILE:]
                ).astype(jnp.bfloat16)
                grads = jnp.dot(pairs[tile], left[tile], preferred_element_type=jnp.float32)
                for j, at in enumerate(places[tile]):
                    sums[pl.ds(at, TILE), :] += grads[j * TILE : (j + 1) * TILE]

        def source_step(source, carry):
            lengths = [meta[source, tile, slots] for tile in range(tiles_each)]
            longest = functools.reduce(jnp.maximum, lengths)
            for count in range(1, slots + 1):
                pl.when(longest == count)(functools.partial(step, source, lengths, count))
            return carry

        lax.fori_loop(0, sources, source_step, 0)
        for r in range(count):
            for i in range(parts):
                fact_outs[r // ys][i * ys + r % ys] = fact_out[r * parts + i]
        if last:
            factor = jnp.where(lane_is((table_rows, LANES), odd), SCALE, 1.0)
            own_out[...] = sums[:table_rows] * factor
            for k in range(1, shares):
                share_outs[k - 1][...] = (
                    sums[k * table_rows : (k + 1) * table_rows] * factor
                ).astype(jnp.bfloat16)

    outs = [bf16(parts * ys, rows, LANES)] * (count // ys)
    wide = jax.ShapeDtypeStruct((shares * table_rows, LANES), jnp.float32)
    scratch = []
    if last:
        outs += [jax.ShapeDtypeStruct((table_rows, LANES), jnp.float32)]
        outs += [bf16(table_rows, LANES)] * (shares - 1)
    else:
        outs += [wide]
    if begin:
        if last:
            scratch += [pltpu.VMEM((shares * table_rows, LANES), jnp.bfloat16)]
        else:
            outs += [bf16(shares * table_rows, LANES)]
    if last:
        scratch += [pltpu.VMEM(wide.shape, wide.dtype)]
    sums_in = [] if begin else [total]
    results = call(
        kernel,
        "attend",
        outs,
        [SMEM] + [VMEM] * (count + len(tables) + len(sums_in)),
        cost=cost,
        vmem=32,
        scratch_shapes=scratch
        + [
            pltpu.VMEM((sources, rows, LANES), jnp.bfloat16),
            pltpu.VMEM((sources, rows, LANES), jnp.bfloat16),
            pltpu.VMEM((sources, META_ROWS, LANES), jnp.int32),
            pltpu.SMEM((sources, META_ROWS, LANES), jnp.int32),
            pltpu.SemaphoreType.DMA,
        ],
    )(place, *facts, *tables, *sums_in)
    return results[: count // ys], results[count // ys :]


def join_planes(place, chunks, xs, cost):
    zs, (count, rows, _) = len(chunks), chunks[0].shape
    ys = count // xs

    def kernel(place, *refs):
        for k in range(zs):
            for n in range(count):
                i, j = divmod(n, ys)
                m = (place[0] ^ i) * ys + (place[4] ^ j)
                refs[zs][m, place[3] ^ k] = refs[zs - 1 - k][n]

    return call(
        kernel, "join_planes", bf16(count, zs, rows, LANES), [SMEM] + [VMEM] * zs, cost=cost
    )(place, *chunks[::-1])


def unpack_fact(parts, xs):
    planes, zs, rows, _ = parts.shape
    ys = planes // xs

    def kernel(parts, attended, query_grad):
        for p in range(HEADS // 2):
            span = slice(p * LANES, (p + 1) * LANES)
            x, dim = divmod(2 * p, zs * ys)
            m, z = x * ys + dim % ys, dim // ys
            query_grad[:, span], attended[:, span] = separate(parts[m, z], parts[m + 1, z])

    return call(
        kernel, "unpack_fact", [bf16(rows, HEADS * HEAD_DIM)] * 2, [VMEM], cost=UNPACK_FACT
    )(parts)


def sum_shares(place, own, others, dims, per_fact):
    rows = own.shape[0] // dims

    def kernel(place, own, *refs):
        others_in, outs = refs[: len(others)], refs[len(others) :]
        for r in range(dims):
            at = pl.multiple_of((r ^ (place[1] * per_fact)) * rows, rows)
            total = own[pl.ds(at, rows), :]
            for other in others_in:
                total += other[pl.ds(at, rows), :].astype(jnp.float32)
            outs[r][...] = total.astype(jnp.bfloat16)

    return call(
        kernel, "sum_shares", [bf16(rows, LANES)] * dims, [SMEM] + [VMEM] * (1 + len(others)), cost=2
    )(place, own, *others)


def unpack_dimension(place, chunks, shares, per_fact):
    dims = len(chunks)
    rows = chunks[0].shape[0]

    def kernel(place, *refs):
        key_grad, value_grad = refs[dims:]
        refs = refs[dims - 1 :: -1]
        odd = (place[2] & 1) == 1
        for i in range(dims // 2):
            source = place[2] ^ (2 * i)
            share = (source // per_fact) ^ place[1]
            pair = in_order(odd, (refs[2 * i][...], refs[2 * i + 1][...]))
            at = pl.ds(pl.multiple_of(share * rows, rows), rows)
            span = pl.ds(pl.multiple_of(((source % per_fact) // 2) * LANES, LANES), LANES)
            key_grad[at, span], value_grad[at, span] = separate(*pair)

    return call(
        kernel,
        "unpack_dimension",
        [bf16(shares * rows, per_fact * HEAD_DIM)] * 2,
        [SMEM] + [VMEM] * dims,
        cost=UNPACK_COST,
    )(place, *reversed(chunks))


def by_xor(part, axis, index, count):
    if index == 0:
        return part
    return lax.ppermute(part, axis, [(i, i ^ index) for i in range(count)])


def exchange(chunks, send):
    moved = list(chunks)
    for r in range(len(chunks)):
        moved[r] = send(chunks[r], r)
    return moved


def body(xs, shares, zs, ys, queries, key_rows, value_rows, cotangent, block_lists, tile_lengths):
    dims = zs * ys
    per_fact = dims // shares
    rows, slots = queries.shape[0], block_lists.shape[1]
    x, share, z, y = (lax.axis_index(a) for a in ("x", "share", "z", "y"))
    place = jnp.stack([x, share, z * ys + y, z, y]).astype(jnp.int32)

    def over_dim(chunk, r):
        return by_xor(chunk, ("z", "y"), r, dims)

    def to_columns(chunk, r):
        pairs = [
            (c * dims + d, (d // per_fact) * dims + (d ^ r ^ (c * per_fact)))
            for c in range(shares)
            for d in range(dims)
        ]
        return lax.ppermute(chunk, ("share", "z", "y"), pairs)

    chunks = pack_dimension(place, key_rows, value_rows, dims, shares)
    chunks = exchange(chunks, over_dim)
    table = stack_chunks(chunks, STACK_COST)
    tables = [by_xor(table, "share", k, shares) for k in range(shares)]

    parts = pack_fact(place, queries, cotangent, block_lists, tile_lengths, dims)
    parts = [by_xor(part, "x", k, xs) for k, part in enumerate(parts)]
    facts = merge_fact(parts)
    facts = exchange(facts, over_dim)

    fact_outs, total = [], None
    for start, stop, cost in BATCHES:
        stop = min(stop * dims // 8, dims)
        outs, rest = attend(
            place,
            facts[start * dims // 8 : stop],
            tables,
            total,
            rows,
            slots,
            dims,
            shares,
            ys,
            stop == dims,
            cost,
        )
        fact_outs += outs
        if stop < dims:
            total = rest[0]
            tables = rest[1:] or tables
    own, others = rest[0], rest[1:]

    fact_outs = [by_xor(chunk, "z", k, zs) for k, chunk in enumerate(fact_outs)]
    others = [by_xor(other, "share", k + 1, shares) for k, other in enumerate(others)]
    chunks = sum_shares(place, own, others, dims, per_fact)
    fact_outs[0], *chunks = lax.optimization_barrier((fact_outs[0], *chunks))
    fact_out = join_planes(place, fact_outs, xs, SPLIT_COST)
    fact_out = lax.all_to_all(fact_out, ("x", "y"), split_axis=0, concat_axis=0, tiled=True)
    attended, query_grad = unpack_fact(fact_out, xs)

    grads = exchange(chunks, to_columns)
    key_grad, value_grad = unpack_dimension(place, grads, shares, per_fact)
    return attended, query_grad, key_grad, value_grad


def solution(mesh):
    facts, dims = mesh.shape["fact"], mesh.shape["dim"]
    xs = HEADS // dims
    shares = facts // xs
    ys = dims // PLANES
    every = ("x", "share", "z", "y")
    fine = Mesh(mesh.devices.reshape(xs, shares, PLANES, ys), every)
    owner, columns = ("z", "y"), ("x", "share")
    in_specs = (
        P(every, None),
        P(owner, None),
        P(owner, None),
        P(every, None),
        P(every, None),
        P(every),
    )
    out_specs = (
        P(every, None),
        P(every, None),
        P(owner, columns),
        P(owner, columns),
    )
    return jax.shard_map(
        functools.partial(body, xs, shares, PLANES, ys),
        mesh=fine,
        in_specs=in_specs,
        out_specs=out_specs,
        check_vma=False,
    )
```

```python
import functools

import jax
import jax.numpy as jnp
from jax import lax
from jax.experimental import pallas as pl
from jax.experimental.pallas import tpu as pltpu
from jax.sharding import Mesh, PartitionSpec as P

HEADS = 16
HEAD_DIM = 64
TILE = 128
LANES = 2 * HEAD_DIM
META_ROWS = 16
LOG2E = 1.4426950408889634
SCALE = HEAD_DIM ** (-0.5)
NEG_FILL = -1e30
PEAK = 1.15e9
MIB = 1024 * 1024
BATCHES = ((0, 4, 0), (4, 6, 0), (6, 8, 60))
SPLIT_COST = 0
UNPACK_FACT = 2
PLANES = 4
COUNTS = (1, 2, 3, 5, 8)
GROUP = 4
STACK_COST = 2
UNPACK_COST = 5

SMEM = pl.BlockSpec(memory_space=pltpu.SMEM)
VMEM = pl.BlockSpec(memory_space=pltpu.VMEM)


def call(kernel, name, out_shape, in_specs, *, cost, vmem=24, **more):
    return pl.pallas_call(
        kernel,
        out_shape=out_shape,
        in_specs=in_specs,
        out_specs=jax.tree.map(lambda _: VMEM, out_shape),
        compiler_params=pltpu.CompilerParams(vmem_limit_bytes=vmem * MIB),
        cost_estimate=pl.CostEstimate(
            flops=int(cost * PEAK), bytes_accessed=0, transcendentals=0
        ),
        name=name,
        **more,
    )


def bf16(*shape):
    return jax.ShapeDtypeStruct(shape, jnp.bfloat16)


def low_lanes(shape):
    return lax.broadcasted_iota(jnp.int32, shape, len(shape) - 1) < HEAD_DIM


def swap_halves(x):
    return jnp.concatenate([x[:, HEAD_DIM:], x[:, :HEAD_DIM]], axis=1)


def interleave(first, second):
    low = low_lanes(first.shape)
    swapped = swap_halves(second)
    return jnp.where(low, first, swapped), jnp.where(low, swapped, first)


def separate(even, odd):
    low = low_lanes(even.shape)
    return jnp.where(low, even, odd), swap_halves(jnp.where(low, odd, even))


def lane_is(shape, odd):
    return (lax.broadcasted_iota(jnp.int32, shape, len(shape) - 1) // HEAD_DIM) == odd


def in_order(odd, pair):
    a, b = pair
    return jnp.where(odd, b, a), jnp.where(odd, a, b)


def pair_lanes(base, place, i):
    return pl.ds(pl.multiple_of((base + ((place[2] >> 1) ^ i)) * LANES, LANES), LANES)


def pack_dimension(key_rows, value_rows, dims, shares, ys):
    rows = key_rows.shape[0] // shares
    pairs = dims // 2

    def kernel(keys_in, values_in, *refs):
        outs, (keys, values, sems) = refs[:dims], refs[dims:]
        x, share, z, y = (lax.axis_index(a) for a in ("x", "share", "z", "y"))
        place = (x, share, z * ys + y)
        odd = (place[2] & 1) == 1
        at = pl.ds(pl.multiple_of(place[1] * rows, rows), rows)

        def copies(i):
            span = pair_lanes(place[0] * pairs, place, i)
            return (
                pltpu.make_async_copy(keys_in.at[at, span], keys.at[i], sems.at[0, i]),
                pltpu.make_async_copy(values_in.at[at, span], values.at[i], sems.at[1, i]),
            )

        for i in range(pairs):
            for copy in copies(i):
                copy.start()
        for i in range(pairs):
            for copy in copies(i):
                copy.wait()
            outs[2 * i][...], outs[2 * i + 1][...] = in_order(
                odd, interleave(keys[i], values[i])
            )

    anywhere = pl.BlockSpec(memory_space=pl.ANY)
    block = pltpu.VMEM((pairs, rows, LANES), jnp.bfloat16)
    return call(
        kernel,
        "pack_dimension",
        [bf16(rows, LANES)] * dims,
        [anywhere, anywhere],
        cost=0,
        vmem=60,
        scratch_shapes=[block, block, pltpu.SemaphoreType.DMA((2, pairs))],
    )(key_rows, value_rows)


def pack_fact(place, queries, cotangent, block_lists, tile_lengths, dims):
    rows = queries.shape[0]
    tiles, slots = block_lists.shape
    parts = HEADS // dims

    def kernel(place, queries, cotangent, block_lists, tile_lengths, *refs):
        *outs, words = refs
        odd = (place[2] & 1) == 1
        words[...] = jnp.zeros_like(words)
        words[:tiles, :slots] = block_lists[...]
        words[:tiles, slots : slots + 1] = tile_lengths[...]
        meta = words[...].astype(jnp.float32).astype(jnp.bfloat16)
        for k in range(parts):
            base = (place[0] ^ k) * (dims // 2)
            for i in range(dims // 2):
                span = pair_lanes(base, place, i)
                pair = in_order(odd, interleave(queries[:, span], cotangent[:, span]))
                for s in range(2):
                    outs[k][2 * i + s, :rows, :] = pair[s]
                    outs[k][2 * i + s, rows:, :] = meta

    return call(
        kernel,
        "pack_fact",
        [bf16(dims, rows + META_ROWS, LANES)] * parts,
        [SMEM, VMEM, VMEM, VMEM, VMEM],
        cost=1,
        scratch_shapes=[pltpu.VMEM((META_ROWS, LANES), jnp.int32)],
    )(place, queries, cotangent, block_lists, tile_lengths[:, None])


def merge_fact(parts):
    dims, rows, _ = parts[0].shape

    def kernel(*refs):
        for r in range(dims):
            for k in range(len(parts)):
                refs[len(parts) + r][k] = refs[k][r]

    return call(
        kernel, "merge_fact", [bf16(len(parts), rows, LANES)] * dims, [VMEM] * len(parts), cost=2
    )(*parts)


def stack_chunks(chunks, cost):
    rows = chunks[0].shape[0]

    def kernel(*refs):
        for r, chunk in enumerate(refs[:-1]):
            refs[-1][r * rows : (r + 1) * rows, :] = chunk[...]

    return call(
        kernel, "stack_chunks", bf16(len(chunks) * rows, LANES), [VMEM] * len(chunks), cost=cost
    )(*chunks)


def attend(place, facts, tables, total, rows, slots, dims, shares, ys, last, cost):
    count = len(facts)
    parts = facts[0].shape[0]
    sources = count * parts
    table_rows = sum(t.shape[0] for t in tables) // shares
    owner_blocks = table_rows // TILE // dims
    tiles_each = rows // TILE
    begin = total is None

    def kernel(place, *refs):
        refs = list(refs)

        def take(n):
            taken = refs[:n]
            del refs[:n]
            return taken

        facts_in = take(count)
        tables_in = take(len(tables))
        (total_in,) = take(1) if not begin else (None,)
        fact_outs = take(count // ys)
        if last:
            (own_out,), share_outs = take(1), take(shares - 1)
        else:
            (sums_out,) = take(1)
        (table,) = take(1) if begin else tables_in
        (sums,) = take(1) if last else (sums_out,)
        fact, fact_out, words, meta, order, sem = refs
        odd = place[2] & 1
        for r in range(count):
            words[r * parts : (r + 1) * parts] = (
                facts_in[r][:, rows:, :].astype(jnp.float32).astype(jnp.int32)
            )
        copy = pltpu.make_async_copy(words, meta, sem)
        copy.start()
        for r in range(count):
            fact[r * parts : (r + 1) * parts] = facts_in[r][:, :rows, :]
        if begin:
            for k in range(shares):
                table[k * table_rows : (k + 1) * table_rows, :] = tables_in[k][...]
            sums[...] = jnp.zeros_like(sums)
        else:
            sums[...] = total_in[...]
        copy.wait()
        first = lane_is((TILE, LANES), odd)

        def row_of(block):
            owner, place_in = block // (shares * owner_blocks), block % (shares * owner_blocks)
            share, at = place_in // owner_blocks, place_in % owner_blocks
            index = ((share ^ place[1]) * dims + (owner ^ place[2])) * owner_blocks + at
            return pl.multiple_of(index * TILE, TILE)

        tiles = sources * tiles_each
        lengths = [meta[t // tiles_each, t % tiles_each, slots] for t in range(tiles)]
        ranks = [jnp.int32(0)] * tiles
        for t in range(tiles):
            for u in range(t):
                ahead = (lengths[u] >= lengths[t]).astype(jnp.int32)
                ranks[t] += ahead
                ranks[u] += 1 - ahead
        for t in range(tiles):
            order[ranks[t]] = t

        def step(index, longest):
            chosen = [order[index * GROUP + g] for g in range(GROUP)]
            spots = [(t // tiles_each, pl.multiple_of(t % tiles_each * TILE, TILE)) for t in chosen]
            left, places, live, pairs = [], [], [], []
            for t, (source, start) in zip(chosen, spots):
                both = fact[source, pl.ds(start, TILE), :]
                zero = jnp.zeros_like(both)
                left.append(
                    jnp.concatenate(
                        [jnp.where(first, both, zero), jnp.where(first, zero, both)], axis=0
                    )
                )
                tile = t % tiles_each
                places.append([row_of(meta[source, tile, j]) for j in range(longest)])
                live.append(meta[source, tile, slots])
            kept = []
            for g in range(GROUP):
                kv = jnp.concatenate([table[pl.ds(at, TILE), :] for at in places[g]], axis=0)
                products = lax.dot_general(
                    kv, left[g], (((1,), (1,)), ((), ())), preferred_element_type=jnp.float32
                )
                scores = products[:, :TILE] * (SCALE * LOG2E)
                if longest > 1:
                    scores = jnp.concatenate(
                        [scores[:TILE]]
                        + [
                            jnp.where(live[g] > j, scores[j * TILE : (j + 1) * TILE], NEG_FILL)
                            for j in range(1, longest)
                        ],
                        axis=0,
                    )
                dweights = products[:, TILE:]
                terms = jnp.exp2(scores - jnp.max(scores, axis=0, keepdims=True))
                weights = terms * (1.0 / jnp.sum(terms, axis=0, keepdims=True))
                row_delta = jnp.sum(weights * dweights, axis=0, keepdims=True)
                dscores = weights * (dweights - row_delta)
                kept.append(kv)
                pairs.append(
                    jnp.concatenate(
                        [dscores.astype(jnp.bfloat16), weights.astype(jnp.bfloat16)], axis=1
                    )
                )
            for g, (source, start) in enumerate(spots):
                out = lax.dot_general(
                    pairs[g], kept[g], (((0,), (0,)), ((), ())), preferred_element_type=jnp.float32
                )
                fact_out[source, pl.ds(start, TILE), :] = jnp.where(
                    first, out[:TILE] * SCALE, out[TILE:]
                ).astype(jnp.bfloat16)
                grads = jnp.dot(pairs[g], left[g], preferred_element_type=jnp.float32)
                for j, at in enumerate(places[g]):
                    sums[pl.ds(at, TILE), :] += grads[j * TILE : (j + 1) * TILE]

        def group_step(index, carry):
            first_tile = order[index * GROUP]
            longest = meta[first_tile // tiles_each, first_tile % tiles_each, slots]
            for below, length in zip((0,) + COUNTS, COUNTS):
                pl.when((longest > below) & (longest <= length))(
                    functools.partial(step, index, length)
                )
            return carry

        lax.fori_loop(0, tiles // GROUP, group_step, 0)
        for r in range(count):
            for i in range(parts):
                fact_outs[r // ys][i * ys + r % ys] = fact_out[r * parts + i]
        if last:
            factor = jnp.where(lane_is((table_rows, LANES), odd), SCALE, 1.0)
            own_out[...] = sums[:table_rows] * factor
            for k in range(1, shares):
                share_outs[k - 1][...] = (
                    sums[k * table_rows : (k + 1) * table_rows] * factor
                ).astype(jnp.bfloat16)

    outs = [bf16(parts * ys, rows, LANES)] * (count // ys)
    wide = jax.ShapeDtypeStruct((shares * table_rows, LANES), jnp.float32)
    scratch = []
    if last:
        outs += [jax.ShapeDtypeStruct((table_rows, LANES), jnp.float32)]
        outs += [bf16(table_rows, LANES)] * (shares - 1)
    else:
        outs += [wide]
    if begin:
        if last:
            scratch += [pltpu.VMEM((shares * table_rows, LANES), jnp.bfloat16)]
        else:
            outs += [bf16(shares * table_rows, LANES)]
    if last:
        scratch += [pltpu.VMEM(wide.shape, wide.dtype)]
    sums_in = [] if begin else [total]
    results = call(
        kernel,
        "attend",
        outs,
        [SMEM] + [VMEM] * (count + len(tables) + len(sums_in)),
        cost=cost,
        vmem=32,
        scratch_shapes=scratch
        + [
            pltpu.VMEM((sources, rows, LANES), jnp.bfloat16),
            pltpu.VMEM((sources, rows, LANES), jnp.bfloat16),
            pltpu.VMEM((sources, META_ROWS, LANES), jnp.int32),
            pltpu.SMEM((sources, META_ROWS, LANES), jnp.int32),
            pltpu.SMEM((sources * tiles_each,), jnp.int32),
            pltpu.SemaphoreType.DMA,
        ],
    )(place, *facts, *tables, *sums_in)
    return results[: count // ys], results[count // ys :]


def join_planes(place, chunks, xs, cost):
    zs, (count, rows, _) = len(chunks), chunks[0].shape
    ys = count // xs

    def kernel(place, *refs):
        for k in range(zs):
            for n in range(count):
                i, j = divmod(n, ys)
                m = (place[0] ^ i) * ys + (place[4] ^ j)
                refs[zs][m, place[3] ^ k] = refs[zs - 1 - k][n]

    return call(
        kernel, "join_planes", bf16(count, zs, rows, LANES), [SMEM] + [VMEM] * zs, cost=cost
    )(place, *chunks[::-1])


def unpack_fact(parts, xs):
    planes, zs, rows, _ = parts.shape
    ys = planes // xs

    def kernel(parts, attended, query_grad):
        for p in range(HEADS // 2):
            span = slice(p * LANES, (p + 1) * LANES)
            x, dim = divmod(2 * p, zs * ys)
            m, z = x * ys + dim % ys, dim // ys
            query_grad[:, span], attended[:, span] = separate(parts[m, z], parts[m + 1, z])

    return call(
        kernel, "unpack_fact", [bf16(rows, HEADS * HEAD_DIM)] * 2, [VMEM], cost=UNPACK_FACT
    )(parts)


def sum_shares(place, own, others, dims, per_fact):
    rows = own.shape[0] // dims

    def kernel(place, own, *refs):
        others_in, outs = refs[: len(others)], refs[len(others) :]
        for r in range(dims):
            at = pl.multiple_of((r ^ (place[1] * per_fact)) * rows, rows)
            total = own[pl.ds(at, rows), :]
            for other in others_in:
                total += other[pl.ds(at, rows), :].astype(jnp.float32)
            outs[r][...] = total.astype(jnp.bfloat16)

    return call(
        kernel, "sum_shares", [bf16(rows, LANES)] * dims, [SMEM] + [VMEM] * (1 + len(others)), cost=2
    )(place, own, *others)


def unpack_dimension(place, chunks, shares, per_fact):
    dims = len(chunks)
    rows = chunks[0].shape[0]

    def kernel(place, *refs):
        key_grad, value_grad = refs[dims:]
        refs = refs[dims - 1 :: -1]
        odd = (place[2] & 1) == 1
        for i in range(dims // 2):
            source = place[2] ^ (2 * i)
            share = (source // per_fact) ^ place[1]
            pair = in_order(odd, (refs[2 * i][...], refs[2 * i + 1][...]))
            at = pl.ds(pl.multiple_of(share * rows, rows), rows)
            span = pl.ds(pl.multiple_of(((source % per_fact) // 2) * LANES, LANES), LANES)
            key_grad[at, span], value_grad[at, span] = separate(*pair)

    return call(
        kernel,
        "unpack_dimension",
        [bf16(shares * rows, per_fact * HEAD_DIM)] * 2,
        [SMEM] + [VMEM] * dims,
        cost=UNPACK_COST,
    )(place, *reversed(chunks))


def by_xor(part, axis, index, count):
    if index == 0:
        return part
    return lax.ppermute(part, axis, [(i, i ^ index) for i in range(count)])


def exchange(chunks, send):
    moved = list(chunks)
    for r in range(len(chunks)):
        moved[r] = send(chunks[r], r)
    return moved


def body(xs, shares, zs, ys, queries, key_rows, value_rows, cotangent, block_lists, tile_lengths):
    dims = zs * ys
    per_fact = dims // shares
    rows, slots = queries.shape[0], block_lists.shape[1]
    x, share, z, y = (lax.axis_index(a) for a in ("x", "share", "z", "y"))
    place = jnp.stack([x, share, z * ys + y, z, y]).astype(jnp.int32)

    def over_dim(chunk, r):
        return by_xor(chunk, ("z", "y"), r, dims)

    def to_columns(chunk, r):
        pairs = [
            (c * dims + d, (d // per_fact) * dims + (d ^ r ^ (c * per_fact)))
            for c in range(shares)
            for d in range(dims)
        ]
        return lax.ppermute(chunk, ("share", "z", "y"), pairs)

    chunks = pack_dimension(key_rows, value_rows, dims, shares, ys)
    chunks = exchange(chunks, over_dim)
    table = stack_chunks(chunks, STACK_COST)
    tables = [by_xor(table, "share", k, shares) for k in range(shares)]

    parts = pack_fact(place, queries, cotangent, block_lists, tile_lengths, dims)
    parts = [by_xor(part, "x", k, xs) for k, part in enumerate(parts)]
    facts = merge_fact(parts)
    facts = exchange(facts, over_dim)

    fact_outs, total = [], None
    for start, stop, cost in BATCHES:
        stop = min(stop * dims // 8, dims)
        outs, rest = attend(
            place,
            facts[start * dims // 8 : stop],
            tables,
            total,
            rows,
            slots,
            dims,
            shares,
            ys,
            stop == dims,
            cost,
        )
        fact_outs += outs
        if stop < dims:
            total = rest[0]
            tables = rest[1:] or tables
    own, others = rest[0], rest[1:]

    fact_outs = [by_xor(chunk, "z", k, zs) for k, chunk in enumerate(fact_outs)]
    others = [by_xor(other, "share", k + 1, shares) for k, other in enumerate(others)]
    chunks = sum_shares(place, own, others, dims, per_fact)
    fact_outs[0], *chunks = lax.optimization_barrier((fact_outs[0], *chunks))
    fact_out = join_planes(place, fact_outs, xs, SPLIT_COST)
    fact_out = lax.all_to_all(fact_out, ("x", "y"), split_axis=0, concat_axis=0, tiled=True)
    attended, query_grad = unpack_fact(fact_out, xs)

    grads = exchange(chunks, to_columns)
    key_grad, value_grad = unpack_dimension(place, grads, shares, per_fact)
    return attended, query_grad, key_grad, value_grad


def solution(mesh):
    facts, dims = mesh.shape["fact"], mesh.shape["dim"]
    xs = HEADS // dims
    shares = facts // xs
    ys = dims // PLANES
    every = ("x", "share", "z", "y")
    fine = Mesh(mesh.devices.reshape(xs, shares, PLANES, ys), every)
    owner, columns = ("z", "y"), ("x", "share")
    in_specs = (
        P(every, None),
        P(owner, None),
        P(owner, None),
        P(every, None),
        P(every, None),
        P(every),
    )
    out_specs = (
        P(every, None),
        P(every, None),
        P(owner, columns),
        P(owner, columns),
    )
    return jax.shard_map(
        functools.partial(body, xs, shares, PLANES, ys),
        mesh=fine,
        in_specs=in_specs,
        out_specs=out_specs,
        check_vma=False,
    )
```

```python
import functools

import jax
import jax.numpy as jnp
from jax import lax
from jax.experimental import pallas as pl
from jax.experimental.pallas import tpu as pltpu
from jax.sharding import Mesh, PartitionSpec as P

HEADS = 16
HEAD_DIM = 64
TILE = 128
LANES = 2 * HEAD_DIM
META_ROWS = 16
LOG2E = 1.4426950408889634
SCALE = HEAD_DIM ** (-0.5)
NEG_FILL = -1e30
PEAK = 1.15e9
MIB = 1024 * 1024
BATCHES = ((0, 4, 0), (4, 6, 0), (6, 8, 60))
SPLIT_COST = 0
UNPACK_FACT = 2
PLANES = 4
COUNTS = (1, 2, 3, 5, 8)
GROUP = 4
STACK_COST = 2
UNPACK_COST = 5

SMEM = pl.BlockSpec(memory_space=pltpu.SMEM)
VMEM = pl.BlockSpec(memory_space=pltpu.VMEM)


def call(kernel, name, out_shape, in_specs, *, cost, vmem=24, **more):
    return pl.pallas_call(
        kernel,
        out_shape=out_shape,
        in_specs=in_specs,
        out_specs=jax.tree.map(lambda _: VMEM, out_shape),
        compiler_params=pltpu.CompilerParams(vmem_limit_bytes=vmem * MIB),
        cost_estimate=pl.CostEstimate(
            flops=int(cost * PEAK), bytes_accessed=0, transcendentals=0
        ),
        name=name,
        **more,
    )


def bf16(*shape):
    return jax.ShapeDtypeStruct(shape, jnp.bfloat16)


def low_lanes(shape):
    return lax.broadcasted_iota(jnp.int32, shape, len(shape) - 1) < HEAD_DIM


def swap_halves(x):
    return jnp.concatenate([x[:, HEAD_DIM:], x[:, :HEAD_DIM]], axis=1)


def interleave(first, second):
    low = low_lanes(first.shape)
    swapped = swap_halves(second)
    return jnp.where(low, first, swapped), jnp.where(low, swapped, first)


def separate(even, odd):
    low = low_lanes(even.shape)
    return jnp.where(low, even, odd), swap_halves(jnp.where(low, odd, even))


def lane_is(shape, odd):
    return (lax.broadcasted_iota(jnp.int32, shape, len(shape) - 1) // HEAD_DIM) == odd


def in_order(odd, pair):
    a, b = pair
    return jnp.where(odd, b, a), jnp.where(odd, a, b)


def pair_lanes(base, place, i):
    return pl.ds(pl.multiple_of((base + ((place[2] >> 1) ^ i)) * LANES, LANES), LANES)


def pack_dimension(key_rows, value_rows, dims, shares, ys):
    rows = key_rows.shape[0] // shares
    pairs = dims // 2

    def kernel(keys_in, values_in, *refs):
        outs, (keys, values, sems) = refs[:dims], refs[dims:]
        x, share, z, y = (lax.axis_index(a) for a in ("x", "share", "z", "y"))
        place = (x, share, z * ys + y)
        odd = (place[2] & 1) == 1
        at = pl.ds(pl.multiple_of(place[1] * rows, rows), rows)

        def copies(i):
            span = pair_lanes(place[0] * pairs, place, i)
            return (
                pltpu.make_async_copy(keys_in.at[at, span], keys.at[i], sems.at[0, i]),
                pltpu.make_async_copy(values_in.at[at, span], values.at[i], sems.at[1, i]),
            )

        for i in range(pairs):
            for copy in copies(i):
                copy.start()
        for i in range(pairs):
            for copy in copies(i):
                copy.wait()
            outs[2 * i][...], outs[2 * i + 1][...] = in_order(
                odd, interleave(keys[i], values[i])
            )

    anywhere = pl.BlockSpec(memory_space=pl.ANY)
    block = pltpu.VMEM((pairs, rows, LANES), jnp.bfloat16)
    return call(
        kernel,
        "pack_dimension",
        [bf16(rows, LANES)] * dims,
        [anywhere, anywhere],
        cost=0,
        vmem=60,
        scratch_shapes=[block, block, pltpu.SemaphoreType.DMA((2, pairs))],
    )(key_rows, value_rows)


def pack_fact(place, queries, cotangent, block_lists, tile_lengths, dims):
    rows = queries.shape[0]
    tiles, slots = block_lists.shape
    parts = HEADS // dims

    def kernel(place, queries, cotangent, block_lists, tile_lengths, *refs):
        *outs, words = refs
        odd = (place[2] & 1) == 1
        for k in range(parts):
            lists = slice(k * tiles, (k + 1) * tiles)
            words[...] = jnp.zeros_like(words)
            words[lists, :slots] = block_lists[...]
            words[lists, slots : slots + 1] = tile_lengths[...]
            meta = words[...].astype(jnp.float32).astype(jnp.bfloat16)
            base = (place[0] ^ k) * (dims // 2)
            for i in range(dims // 2):
                span = pair_lanes(base, place, i)
                pair = in_order(odd, interleave(queries[:, span], cotangent[:, span]))
                for s in range(2):
                    outs[k][2 * i + s, :rows, :] = pair[s]
                    outs[k][2 * i + s, rows:, :] = meta

    return call(
        kernel,
        "pack_fact",
        [bf16(dims, rows + META_ROWS, LANES)] * parts,
        [SMEM, VMEM, VMEM, VMEM, VMEM],
        cost=1,
        scratch_shapes=[pltpu.VMEM((META_ROWS, LANES), jnp.int32)],
    )(place, queries, cotangent, block_lists, tile_lengths[:, None])


def merge_fact(parts):
    dims, rows, _ = parts[0].shape
    rows -= META_ROWS
    count = len(parts)

    def kernel(*refs):
        for r in range(dims):
            out = refs[count + r]
            for k in range(count):
                out[k * rows : (k + 1) * rows, :] = refs[k][r, :rows, :]
            lists = [refs[k][r, rows:, :].astype(jnp.float32) for k in range(count)]
            out[count * rows :, :] = functools.reduce(jnp.add, lists).astype(jnp.bfloat16)

    return call(
        kernel,
        "merge_fact",
        [bf16(count * rows + META_ROWS, LANES)] * dims,
        [VMEM] * count,
        cost=4,
    )(*parts)


def stack_chunks(chunks, cost):
    rows = chunks[0].shape[0]

    def kernel(*refs):
        for r, chunk in enumerate(refs[:-1]):
            refs[-1][r * rows : (r + 1) * rows, :] = chunk[...]

    return call(
        kernel, "stack_chunks", bf16(len(chunks) * rows, LANES), [VMEM] * len(chunks), cost=cost
    )(*chunks)


def attend(place, facts, tables, total, rows, slots, dims, shares, ys, last, cost):
    count = len(facts)
    parts = (facts[0].shape[0] - META_ROWS) // rows
    sources = count * parts
    table_rows = sum(t.shape[0] for t in tables) // shares
    owner_blocks = table_rows // TILE // dims
    tiles_each = rows // TILE
    begin = total is None

    def kernel(place, *refs):
        refs = list(refs)

        def take(n):
            taken = refs[:n]
            del refs[:n]
            return taken

        facts_in = take(count)
        tables_in = take(len(tables))
        (total_in,) = take(1) if not begin else (None,)
        fact_outs = take(count // ys)
        if last:
            (own_out,), share_outs = take(1), take(shares - 1)
        else:
            (sums_out,) = take(1)
        (table,) = take(1) if begin else tables_in
        (sums,) = take(1) if last else (sums_out,)
        fact, fact_out, words, meta, order, sem = refs
        odd = place[2] & 1
        for r in range(count):
            words[r] = facts_in[r][parts * rows :, :].astype(jnp.float32).astype(jnp.int32)
        copy = pltpu.make_async_copy(words, meta, sem)
        copy.start()
        for r in range(count):
            for i in range(parts):
                fact[r * parts + i] = facts_in[r][i * rows : (i + 1) * rows, :]
        if begin:
            for k in range(shares):
                table[k * table_rows : (k + 1) * table_rows, :] = tables_in[k][...]
            sums[...] = jnp.zeros_like(sums)
        else:
            sums[...] = total_in[...]
        copy.wait()
        first = lane_is((TILE, LANES), odd)

        def row_of(block):
            owner, place_in = block // (shares * owner_blocks), block % (shares * owner_blocks)
            share, at = place_in // owner_blocks, place_in % owner_blocks
            index = ((share ^ place[1]) * dims + (owner ^ place[2])) * owner_blocks + at
            return pl.multiple_of(index * TILE, TILE)

        tiles = sources * tiles_each

        def word(t, j):
            return meta[t // (parts * tiles_each), t % (parts * tiles_each), j]

        lengths = [word(t, slots) for t in range(tiles)]
        ranks = [jnp.int32(0)] * tiles
        for t in range(tiles):
            for u in range(t):
                ahead = (lengths[u] >= lengths[t]).astype(jnp.int32)
                ranks[t] += ahead
                ranks[u] += 1 - ahead
        for t in range(tiles):
            order[ranks[t]] = t

        def step(index, longest):
            chosen = [order[index * GROUP + g] for g in range(GROUP)]
            spots = [(t // tiles_each, pl.multiple_of(t % tiles_each * TILE, TILE)) for t in chosen]
            left, places, live, pairs = [], [], [], []
            for t, (source, start) in zip(chosen, spots):
                both = fact[source, pl.ds(start, TILE), :]
                zero = jnp.zeros_like(both)
                left.append(
                    jnp.concatenate(
                        [jnp.where(first, both, zero), jnp.where(first, zero, both)], axis=0
                    )
                )
                places.append([row_of(word(t, j)) for j in range(longest)])
                live.append(word(t, slots))
            kept = []
            for g in range(GROUP):
                kv = jnp.concatenate([table[pl.ds(at, TILE), :] for at in places[g]], axis=0)
                products = lax.dot_general(
                    kv, left[g], (((1,), (1,)), ((), ())), preferred_element_type=jnp.float32
                )
                scores = products[:, :TILE] * (SCALE * LOG2E)
                if longest > 1:
                    scores = jnp.concatenate(
                        [scores[:TILE]]
                        + [
                            jnp.where(live[g] > j, scores[j * TILE : (j + 1) * TILE], NEG_FILL)
                            for j in range(1, longest)
                        ],
                        axis=0,
                    )
                dweights = products[:, TILE:]
                terms = jnp.exp2(scores - jnp.max(scores, axis=0, keepdims=True))
                weights = terms * (1.0 / jnp.sum(terms, axis=0, keepdims=True))
                row_delta = jnp.sum(weights * dweights, axis=0, keepdims=True)
                dscores = weights * (dweights - row_delta)
                kept.append(kv)
                pairs.append(
                    jnp.concatenate(
                        [dscores.astype(jnp.bfloat16), weights.astype(jnp.bfloat16)], axis=1
                    )
                )
            for g, (source, start) in enumerate(spots):
                out = lax.dot_general(
                    pairs[g], kept[g], (((0,), (0,)), ((), ())), preferred_element_type=jnp.float32
                )
                fact_out[source, pl.ds(start, TILE), :] = jnp.where(
                    first, out[:TILE] * SCALE, out[TILE:]
                ).astype(jnp.bfloat16)
                grads = jnp.dot(pairs[g], left[g], preferred_element_type=jnp.float32)
                for j, at in enumerate(places[g]):
                    sums[pl.ds(at, TILE), :] += grads[j * TILE : (j + 1) * TILE]

        def group_step(index, carry):
            longest = word(order[index * GROUP], slots)
            for below, length in zip((0,) + COUNTS, COUNTS):
                pl.when((longest > below) & (longest <= length))(
                    functools.partial(step, index, length)
                )
            return carry

        lax.fori_loop(0, tiles // GROUP, group_step, 0)
        for r in range(count):
            for i in range(parts):
                fact_outs[r // ys][i * ys + r % ys] = fact_out[r * parts + i]
        if last:
            factor = jnp.where(lane_is((table_rows, LANES), odd), SCALE, 1.0)
            own_out[...] = sums[:table_rows] * factor
            for k in range(1, shares):
                share_outs[k - 1][...] = (
                    sums[k * table_rows : (k + 1) * table_rows] * factor
                ).astype(jnp.bfloat16)

    outs = [bf16(parts * ys, rows, LANES)] * (count // ys)
    wide = jax.ShapeDtypeStruct((shares * table_rows, LANES), jnp.float32)
    scratch = []
    if last:
        outs += [jax.ShapeDtypeStruct((table_rows, LANES), jnp.float32)]
        outs += [bf16(table_rows, LANES)] * (shares - 1)
    else:
        outs += [wide]
    if begin:
        if last:
            scratch += [pltpu.VMEM((shares * table_rows, LANES), jnp.bfloat16)]
        else:
            outs += [bf16(shares * table_rows, LANES)]
    if last:
        scratch += [pltpu.VMEM(wide.shape, wide.dtype)]
    sums_in = [] if begin else [total]
    results = call(
        kernel,
        "attend",
        outs,
        [SMEM] + [VMEM] * (count + len(tables) + len(sums_in)),
        cost=cost,
        vmem=32,
        scratch_shapes=scratch
        + [
            pltpu.VMEM((sources, rows, LANES), jnp.bfloat16),
            pltpu.VMEM((sources, rows, LANES), jnp.bfloat16),
            pltpu.VMEM((count, META_ROWS, LANES), jnp.int32),
            pltpu.SMEM((count, META_ROWS, LANES), jnp.int32),
            pltpu.SMEM((sources * tiles_each,), jnp.int32),
            pltpu.SemaphoreType.DMA,
        ],
    )(place, *facts, *tables, *sums_in)
    return results[: count // ys], results[count // ys :]


def join_planes(place, chunks, xs, cost):
    zs, (count, rows, _) = len(chunks), chunks[0].shape
    ys = count // xs

    def kernel(place, *refs):
        for k in range(zs):
            for n in range(count):
                i, j = divmod(n, ys)
                m = (place[0] ^ i) * ys + (place[4] ^ j)
                refs[zs][m, place[3] ^ k] = refs[zs - 1 - k][n]

    return call(
        kernel, "join_planes", bf16(count, zs, rows, LANES), [SMEM] + [VMEM] * zs, cost=cost
    )(place, *chunks[::-1])


def unpack_fact(parts, xs):
    planes, zs, rows, _ = parts.shape
    ys = planes // xs

    def kernel(parts, attended, query_grad):
        for p in range(HEADS // 2):
            span = slice(p * LANES, (p + 1) * LANES)
            x, dim = divmod(2 * p, zs * ys)
            m, z = x * ys + dim % ys, dim // ys
            query_grad[:, span], attended[:, span] = separate(parts[m, z], parts[m + 1, z])

    return call(
        kernel, "unpack_fact", [bf16(rows, HEADS * HEAD_DIM)] * 2, [VMEM], cost=UNPACK_FACT
    )(parts)


def sum_shares(place, own, others, dims, per_fact):
    rows = own.shape[0] // dims

    def kernel(place, own, *refs):
        others_in, outs = refs[: len(others)], refs[len(others) :]
        for r in range(dims):
            at = pl.multiple_of((r ^ (place[1] * per_fact)) * rows, rows)
            total = own[pl.ds(at, rows), :]
            for other in others_in:
                total += other[pl.ds(at, rows), :].astype(jnp.float32)
            outs[r][...] = total.astype(jnp.bfloat16)

    return call(
        kernel, "sum_shares", [bf16(rows, LANES)] * dims, [SMEM] + [VMEM] * (1 + len(others)), cost=2
    )(place, own, *others)


def unpack_dimension(place, chunks, shares, per_fact):
    dims = len(chunks)
    rows = chunks[0].shape[0]

    def kernel(place, *refs):
        key_grad, value_grad = refs[dims:]
        refs = refs[dims - 1 :: -1]
        odd = (place[2] & 1) == 1
        for i in range(dims // 2):
            source = place[2] ^ (2 * i)
            share = (source // per_fact) ^ place[1]
            pair = in_order(odd, (refs[2 * i][...], refs[2 * i + 1][...]))
            at = pl.ds(pl.multiple_of(share * rows, rows), rows)
            span = pl.ds(pl.multiple_of(((source % per_fact) // 2) * LANES, LANES), LANES)
            key_grad[at, span], value_grad[at, span] = separate(*pair)

    return call(
        kernel,
        "unpack_dimension",
        [bf16(shares * rows, per_fact * HEAD_DIM)] * 2,
        [SMEM] + [VMEM] * dims,
        cost=UNPACK_COST,
    )(place, *reversed(chunks))


def by_xor(part, axis, index, count):
    if index == 0:
        return part
    return lax.ppermute(part, axis, [(i, i ^ index) for i in range(count)])


def exchange(chunks, send):
    moved = list(chunks)
    for r in range(len(chunks)):
        moved[r] = send(chunks[r], r)
    return moved


def body(xs, shares, zs, ys, queries, key_rows, value_rows, cotangent, block_lists, tile_lengths):
    dims = zs * ys
    per_fact = dims // shares
    rows, slots = queries.shape[0], block_lists.shape[1]
    x, share, z, y = (lax.axis_index(a) for a in ("x", "share", "z", "y"))
    place = jnp.stack([x, share, z * ys + y, z, y]).astype(jnp.int32)

    def over_dim(chunk, r):
        return by_xor(chunk, ("z", "y"), r, dims)

    def to_columns(chunk, r):
        pairs = [
            (c * dims + d, (d // per_fact) * dims + (d ^ r ^ (c * per_fact)))
            for c in range(shares)
            for d in range(dims)
        ]
        return lax.ppermute(chunk, ("share", "z", "y"), pairs)

    chunks = pack_dimension(key_rows, value_rows, dims, shares, ys)
    chunks = exchange(chunks, over_dim)
    table = stack_chunks(chunks, STACK_COST)
    tables = [by_xor(table, "share", k, shares) for k in range(shares)]

    parts = pack_fact(place, queries, cotangent, block_lists, tile_lengths, dims)
    parts = [by_xor(part, "x", k, xs) for k, part in enumerate(parts)]
    facts = merge_fact(parts)
    facts = exchange(facts, over_dim)

    fact_outs, total = [], None
    for start, stop, cost in BATCHES:
        stop = min(stop * dims // 8, dims)
        outs, rest = attend(
            place,
            facts[start * dims // 8 : stop],
            tables,
            total,
            rows,
            slots,
            dims,
            shares,
            ys,
            stop == dims,
            cost,
        )
        fact_outs += outs
        if stop < dims:
            total = rest[0]
            tables = rest[1:] or tables
    own, others = rest[0], rest[1:]

    fact_outs = [by_xor(chunk, "z", k, zs) for k, chunk in enumerate(fact_outs)]
    others = [by_xor(other, "share", k + 1, shares) for k, other in enumerate(others)]
    chunks = sum_shares(place, own, others, dims, per_fact)
    fact_outs[0], *chunks = lax.optimization_barrier((fact_outs[0], *chunks))
    fact_out = join_planes(place, fact_outs, xs, SPLIT_COST)
    fact_out = lax.all_to_all(fact_out, ("x", "y"), split_axis=0, concat_axis=0, tiled=True)
    attended, query_grad = unpack_fact(fact_out, xs)

    grads = exchange(chunks, to_columns)
    key_grad, value_grad = unpack_dimension(place, grads, shares, per_fact)
    return attended, query_grad, key_grad, value_grad


def solution(mesh):
    facts, dims = mesh.shape["fact"], mesh.shape["dim"]
    xs = HEADS // dims
    shares = facts // xs
    ys = dims // PLANES
    every = ("x", "share", "z", "y")
    fine = Mesh(mesh.devices.reshape(xs, shares, PLANES, ys), every)
    owner, columns = ("z", "y"), ("x", "share")
    in_specs = (
        P(every, None),
        P(owner, None),
        P(owner, None),
        P(every, None),
        P(every, None),
        P(every),
    )
    out_specs = (
        P(every, None),
        P(every, None),
        P(owner, columns),
        P(owner, columns),
    )
    return jax.shard_map(
        functools.partial(body, xs, shares, PLANES, ys),
        mesh=fine,
        in_specs=in_specs,
        out_specs=out_specs,
        check_vma=False,
    )
```
